128 devices in a mesh: seq: 32 (over x, z, core), mp: 4 (over y).
Axes of the slice: x: 4, y: 4, z: 4, core: 2. Of those that a mesh axis runs over, the one named last changes fastest.
Arguments:
- block_input: float32 [16384, 1536], P('seq'), may hold values from -6 to 6
- cotangent: float32 [16384, 1536], P('seq'), may hold values from -25 to 25
- norm_gains: float32 [2, 1536], replicated, may hold values from 0.5 to 6
- conv_weight: float32 [3, 1536], P(None, 'mp'), may hold values from -3.5 to 3.5
- in_weight: float32 [1536, 3, 1536], P('seq', None, 'mp'), may hold values from -0.15625 to 0.15625
- out_weight: float32 [1536, 1536], P('mp', 'seq'), may hold values from -0.01953125 to 0.01953125
- gate_weight: float32 [1536, 6912], P('seq', 'mp'), may hold values from -0.15625 to 0.15625
- up_weight: float32 [1536, 6912], P('seq', 'mp'), may hold values from -0.15625 to 0.15625
- down_weight: float32 [6912, 1536], P('mp', 'seq'), may hold values from -0.01953125 to 0.01953125
- in_rows: float32 [1536], P('seq'), may hold values from 311296 to 1245184
- in_cols: float32 [3, 1536], P(None, 'mp'), may hold values from 311296 to 1245184
- out_rows: float32 [1536], P('mp'), may hold values from 21299200 to 85196800
- out_cols: float32 [1536], P('seq'), may hold values from 21299200 to 85196800
- gate_rows: float32 [1536], P('seq'), may hold values from 49152 to 196608
- gate_cols: float32 [6912], P('mp'), may hold values from 49152 to 196608
- up_rows: float32 [1536], P('seq'), may hold values from 49152 to 196608
- up_cols: float32 [6912], P('mp'), may hold values from 49152 to 196608
- down_rows: float32 [6912], P('mp'), may hold values from 753664 to 3014656
- down_cols: float32 [1536], P('seq'), may hold values from 753664 to 3014656
- conv_moment: float32 [3, 1536], P(None, 'mp'), may hold values from 311296 to 1245184
- gain_moment: float32 [2, 1536], replicated, may hold values from 98304 to 655360
Outputs:
- result: float32 [16384, 1536], P('seq')
- input_grad: float32 [16384, 1536], P('seq')
- in_grad: float32 [1536, 3, 1536], P('seq', None, 'mp')
- out_grad: float32 [1536, 1536], P('mp', 'seq')
- gate_grad: float32 [1536, 6912], P('seq', 'mp')
- up_grad: float32 [1536, 6912], P('seq', 'mp')
- down_grad: float32 [6912, 1536], P('mp', 'seq')
- conv_grad: float32 [3, 1536], P(None, 'mp')
- gain_grad: float32 [2, 1536], replicated
- in_new: float32 [1536, 3, 1536], P('seq', None, 'mp')
- out_new: float32 [1536, 1536], P('mp', 'seq')
- gate_new: float32 [1536, 6912], P('seq', 'mp')
- up_new: float32 [1536, 6912], P('seq', 'mp')
- down_new: float32 [6912, 1536], P('mp', 'seq')
- conv_new: float32 [3, 1536], P(None, 'mp')
- gain_new: float32 [2, 1536], replicated
- in_rows_new: float32 [1536], P('seq')
- in_cols_new: float32 [3, 1536], P(None, 'mp')
- out_rows_new: float32 [1536], P('mp')
- out_cols_new: float32 [1536], P('seq')
- gate_rows_new: float32 [1536], P('seq')
- gate_cols_new: float32 [6912], P('mp')
- up_rows_new: float32 [1536], P('seq')
- up_cols_new: float32 [6912], P('mp')
- down_rows_new: float32 [6912], P('mp')
- down_cols_new: float32 [1536], P('seq')
- conv_moment_new: float32 [3, 1536], P(None, 'mp')
- gain_moment_new: float32 [2, 1536], replicated
The draws below stay inside these ranges and needn't reach their ends.
All inputs are finite; a program needn't handle non-finite values.
Results may differ from the reference program's by a relative error of at most 0.028.
Values may be sent and summed in bfloat16 or wider, within the bound.
No kernel may reach another device: no remote copies, remote signals or barrier semaphores. Data moves between devices by JAX's collectives and lax.ppermute only.
A program may use at most 192 MiB of HBM per device.

```python
import math
import jax
import jax.numpy as jnp
from jax import lax

D = 1536
FF = 6912
KERNEL = 3
SEQS = 2
TOKENS = 16384


def draw_cotangent(key, part):
    key = jax.random.fold_in(key, 11)
    place = jnp.arange(TOKENS, dtype=jnp.float32)[:, None] / TOKENS
    values = jnp.clip(jax.random.normal(key, (TOKENS, D), jnp.float32), -5.0, 5.0)
    return (1.0 + 2.0 * place) * values


def draw_norm_gains(key, part):
    key = jax.random.fold_in(key, 23)
    place = jnp.arange(D, dtype=jnp.float32)[None, :] / D
    factor = jax.random.uniform(key, (2, D), jnp.float32, 0.7, 1.3)
    return (1.0 + 2.0 * place) * factor


def levels(stream_key, shape, pieces, smallest, largest):
    def one(axis_at, shards_of):
        draws = jax.random.uniform(jax.random.fold_in(jax.random.fold_in(stream_key, 6), axis_at), (shards_of,), jnp.float32, smallest / len(pieces), largest / len(pieces))
        return jnp.repeat(jnp.exp(draws), shape[axis_at] // shards_of).reshape((-1,) + (1,) * (len(shape) - axis_at - 1))

    gain = one(*pieces[0])
    for cut in pieces[1:]:
        gain = gain * one(*cut)
    return gain


def centred(key, extent, spread, bound, cuts=(), kind=jnp.bfloat16):
    values = jax.random.normal(key, extent, jnp.float32) * spread
    if len(cuts) > 0:
        values = levels(key, extent, cuts, -0.22, 0.18) * values
    return jnp.clip(values, min=-bound, max=bound).astype(kind)


def setup_inputs(seed: int = 0) -> dict:
    keys = jax.random.split(jax.random.key(seed), 22)
    block_input = centred(keys[0], (TOKENS, D), 1.0, 6.0, ((0, 32),), jnp.float32)
    cotangent = draw_cotangent(jax.random.fold_in(keys[21], 71), 0)
    norm_gains = draw_norm_gains(jax.random.fold_in(keys[21], 71), 0)
    conv_weight = centred(keys[3], (KERNEL, D), KERNEL ** -0.5, 3.5, ((1, 4),), jnp.float32)
    in_weight = centred(keys[4], (D, 3, D), D ** -0.5, 0.15625, ((0, 32), (2, 4)), jnp.float32)
    out_weight = centred(keys[5], (D, D), (64 * D) ** -0.5, 0.01953125, ((0, 4), (1, 32)), jnp.float32)
    gate_weight = centred(keys[6], (D, FF), D ** -0.5, 0.15625, ((0, 32), (1, 4)), jnp.float32)
    up_weight = centred(keys[7], (D, FF), D ** -0.5, 0.15625, ((0, 32), (1, 4)), jnp.float32)
    down_weight = centred(keys[8], (FF, D), (16 * FF) ** -0.5, 0.01953125, ((0, 4), (1, 32)), jnp.float32)
    in_rows = jnp.clip(jnp.exp(math.log(1245184) - 1.3862944 * jax.random.uniform(keys[9], (D,), jnp.float32) ** levels(keys[9], (D,), ((0, 32),), -0.2, 0.2)), 311296.0, 1245184)
    in_cols = jnp.clip(jnp.exp(math.log(1245184) - 1.3862944 * jax.random.uniform(keys[10], (3, D), jnp.float32) ** levels(keys[10], (3, D), ((1, 4),), -0.2, 0.2)), 311296.0, 1245184)
    out_rows = jnp.clip(jnp.exp(math.log(85196800) - 1.3862944 * jax.random.uniform(keys[11], (D,), jnp.float32) ** levels(keys[11], (D,), ((0, 4),), -0.2, 0.2)), 21299200, 85196800)
    out_cols = jnp.clip(jnp.exp(math.log(85196800) - 1.3862944 * jax.random.uniform(keys[12], (D,), jnp.float32) ** levels(keys[12], (D,), ((0, 32),), -0.2, 0.2)), 21299200, 85196800)
    gate_rows = jnp.clip(jnp.exp(math.log(196608.0) - 1.3862944 * jax.random.uniform(keys[13], (D,), jnp.float32) ** levels(keys[13], (D,), ((0, 32),), -0.2, 0.2)), 49152.0, 196608.0)
    gate_cols = jnp.clip(jnp.exp(math.log(196608.0) - 1.3862944 * jax.random.uniform(keys[14], (FF,), jnp.float32) ** levels(keys[14], (FF,), ((0, 4),), -0.2, 0.2)), 49152.0, 196608.0)
    up_rows = jnp.clip(jnp.exp(math.log(196608.0) - 1.3862944 * jax.random.uniform(keys[15], (D,), jnp.float32) ** levels(keys[15], (D,), ((0, 32),), -0.2, 0.2)), 49152.0, 196608.0)
    up_cols = jnp.clip(jnp.exp(math.log(196608.0) - 1.3862944 * jax.random.uniform(keys[16], (FF,), jnp.float32) ** levels(keys[16], (FF,), ((0, 4),), -0.2, 0.2)), 49152.0, 196608.0)
    down_rows = jnp.clip(jnp.exp(math.log(3014656) - 1.3862944 * jax.random.uniform(keys[17], (FF,), jnp.float32) ** levels(keys[17], (FF,), ((0, 4),), -0.2, 0.2)), 753664.0, 3014656)
    down_cols = jnp.clip(jnp.exp(math.log(3014656) - 1.3862944 * jax.random.uniform(keys[18], (D,), jnp.float32) ** levels(keys[18], (D,), ((0, 32),), -0.2, 0.2)), 753664.0, 3014656)
    conv_moment = jnp.clip(jnp.exp(math.log(1245184) - 1.3862944 * jax.random.uniform(keys[19], (KERNEL, D), jnp.float32) ** levels(keys[19], (KERNEL, D), ((1, 4),), -0.2, 0.2)), 311296.0, 1245184)
    gain_moment = jnp.clip(jnp.exp(jax.random.uniform(keys[20], (2, D), jnp.float32, math.log(98304.0), math.log(655360.0))), 98304.0, 655360.0)
    return dict(block_input=block_input, cotangent=cotangent, norm_gains=norm_gains, conv_weight=conv_weight, in_weight=in_weight, out_weight=out_weight, gate_weight=gate_weight, up_weight=up_weight, down_weight=down_weight, in_rows=in_rows, in_cols=in_cols, out_rows=out_rows, out_cols=out_cols, gate_rows=gate_rows, gate_cols=gate_cols, up_rows=up_rows, up_cols=up_cols, down_rows=down_rows, down_cols=down_cols, conv_moment=conv_moment, gain_moment=gain_moment)


NORM_EPS = 1e-05
DECAY_RATE = 0.5
SQUARE_EPS = 1e-30
CLIP_LIMIT = 0.2
STEP_RATE = 4.0

@jax.custom_vjp
def low(v):
    return lax.optimization_barrier(v.astype(jnp.bfloat16)).astype(jnp.float32)

@jax.custom_vjp
def low_back(v):
    return v

def low_keep(v):
    return (low(v), None)

def low_pass(kept, grad):
    return (grad,)

def back_keep(v):
    return (v, None)

def back_low(kept, grad):
    return (low(grad),)
low.defvjp(low_keep, low_pass)
low_back.defvjp(back_keep, back_low)

def rms_norm(values, gain_row):
    return values * lax.rsqrt(lax.optimization_barrier(jnp.mean(values * values, axis=1, keepdims=True)) + NORM_EPS) * gain_row

def matmul(left_side, right_side):
    return jnp.dot(left_side, right_side, precision=lax.Precision.HIGHEST, preferred_element_type=jnp.float32)

def forward(block_input, norm_gains, conv_weight, in_weight, out_weight, gate_weight, up_weight, down_weight):
    seq_length = TOKENS // SEQS
    normed = low(rms_norm(block_input, norm_gains[0]))
    projected = low_back(matmul(normed, low(in_weight).reshape(D, 3 * D))).reshape(TOKENS, 3, D)
    product = (projected[:, 0] * projected[:, 2]).reshape(SEQS, seq_length, D)
    padded = jnp.concatenate([jnp.zeros((SEQS, KERNEL - 1, D), jnp.float32), product], axis=1)
    convolved = conv_weight[0] * padded[:, 0:seq_length]
    for offset in range(1, KERNEL):
        convolved = convolved + conv_weight[offset] * padded[:, offset:offset + seq_length]
    convolved = convolved.reshape(TOKENS, D)
    gated = low(projected[:, 1] * convolved)
    branch = low_back(matmul(gated, low(out_weight)))
    middle = block_input + branch
    normed_two = low(rms_norm(middle, norm_gains[1]))
    gate_pre = low_back(matmul(normed_two, low(gate_weight)))
    upward = low_back(matmul(normed_two, low(up_weight)))
    active = low(jax.nn.silu(gate_pre) * upward)
    feed_out = low_back(matmul(active, low(down_weight)))
    return middle + feed_out

def factored(weight, gradient, row_state, col_state):
    squares = gradient * gradient + SQUARE_EPS
    rows_new = DECAY_RATE * row_state + (1.0 - DECAY_RATE) * lax.optimization_barrier(jnp.mean(squares, axis=1))
    cols_new = DECAY_RATE * col_state + (1.0 - DECAY_RATE) * lax.optimization_barrier(jnp.mean(squares, axis=0))
    second = rows_new[:, None] * cols_new[None, :] / jnp.mean(rows_new)
    update = gradient * lax.rsqrt(second)
    update_rms = jnp.sqrt(jnp.mean(update * update))
    weight_rms = jnp.sqrt(jnp.mean(weight * weight))
    return (weight - STEP_RATE * weight_rms * (update / jnp.maximum(1.0, update_rms / CLIP_LIMIT)), rows_new, cols_new)

def unfactored(weight, gradient, moment):
    moment_new = DECAY_RATE * moment + (1.0 - DECAY_RATE) * (gradient * gradient + SQUARE_EPS)
    update = gradient * lax.rsqrt(moment_new)
    update_rms = jnp.sqrt(lax.optimization_barrier(jnp.mean(update * update, axis=1, keepdims=True)))
    weight_rms = jnp.sqrt(lax.optimization_barrier(jnp.mean(weight * weight, axis=1, keepdims=True)))
    return (weight - STEP_RATE * weight_rms * (update / jnp.maximum(1.0, update_rms / CLIP_LIMIT)), moment_new)

def reference(block_input, cotangent, norm_gains, conv_weight, in_weight, out_weight, gate_weight, up_weight, down_weight, in_rows, in_cols, out_rows, out_cols, gate_rows, gate_cols, up_rows, up_cols, down_rows, down_cols, conv_moment, gain_moment):
    result, pullback = jax.vjp(forward, block_input, norm_gains, conv_weight, in_weight, out_weight, gate_weight, up_weight, down_weight)
    input_grad, gain_grad, conv_grad, in_grad, out_grad, gate_grad, up_grad, down_grad = pullback(cotangent)
    in_new, in_rows_new, in_cols_new = factored(in_weight.reshape(D, 3 * D), in_grad.reshape(D, 3 * D), in_rows, in_cols.reshape(3 * D))
    out_new, out_rows_new, out_cols_new = factored(out_weight, out_grad, out_rows, out_cols)
    gate_new, gate_rows_new, gate_cols_new = factored(gate_weight, gate_grad, gate_rows, gate_cols)
    up_new, up_rows_new, up_cols_new = factored(up_weight, up_grad, up_rows, up_cols)
    down_new, down_rows_new, down_cols_new = factored(down_weight, down_grad, down_rows, down_cols)
    conv_new, conv_moment_new = unfactored(conv_weight.reshape(1, KERNEL * D), conv_grad.reshape(1, KERNEL * D), conv_moment.reshape(1, KERNEL * D))
    gain_new, gain_moment_new = unfactored(norm_gains, gain_grad, gain_moment)
    return (result, input_grad, in_grad, out_grad, gate_grad, up_grad, down_grad, conv_grad, gain_grad, in_new.reshape(D, 3, D), out_new, gate_new, up_new, down_new, conv_new.reshape(KERNEL, D), gain_new, in_rows_new, in_cols_new.reshape(3, D), out_rows_new, out_cols_new, gate_rows_new, gate_cols_new, up_rows_new, up_cols_new, down_rows_new, down_cols_new, conv_moment_new.reshape(KERNEL, D), gain_moment_new)
```

```python
import functools

import jax
import jax.numpy as jnp
from jax import lax
from jax.experimental import pallas as pl
from jax.experimental.pallas import tpu as pltpu
from jax.sharding import Mesh
from jax.sharding import PartitionSpec as P

D = 1536
FF = 6912
KERNEL = 3
SEQS = 2

NORM_EPS = 1e-05
DECAY_RATE = 0.5
SQUARE_EPS = 1e-30
CLIP_LIMIT = 0.2
STEP_RATE = 4.0

BF16 = jnp.bfloat16
F32 = jnp.float32
LANES = 128


def send(x, axis, by):
    size = lax.axis_size(axis)
    return lax.ppermute(x, axis, [(i, (i + by) % size) for i in range(size)])


def shifted(x, axis, by):
    size = lax.axis_size(axis)
    pairs = [(i, i + by) for i in range(size) if 0 <= i + by < size]
    return lax.ppermute(x, axis, pairs)


def dot(left_side, right_side, left_axis, right_axis):
    return lax.dot_general(
        left_side,
        right_side,
        (((left_axis,), (right_axis,)), ((), ())),
        preferred_element_type=F32,
    )


def exchange(x, axes):
    return lax.all_to_all(x, axes, split_axis=0, concat_axis=0, tiled=True)


def spread(x, axes):
    return exchange(jnp.broadcast_to(x, (lax.axis_size(axes), *x.shape)), axes)


def halves(x, axis, cut):
    size = x.shape[axis]
    return (
        lax.slice_in_dim(x, 0, cut, axis=axis),
        lax.slice_in_dim(x, cut, size, axis=axis),
    )


def send_turned(x, turned, by):
    pairs = []
    for i in range(32):
        at = [i // 8, i // 2 % 4]
        axis = (1 - i % 2) ^ turned
        at[axis] = (at[axis] + by) % 4
        pairs.append((i, at[0] * 8 + at[1] * 2 + i % 2))
    return lax.ppermute(x, ("x", "z", "core"), pairs)


def gather_near(block, send_by):
    return send_by(block, 1), send_by(block, -1)


def gather_far(block, near, send_by, cut):
    before, after = near
    return block, after, send_by(before[:cut], 1), send_by(after[cut:], -1), before


def ring_gather(block, send_by, cut):
    return gather_far(block, gather_near(block, send_by), send_by, cut)


def gather_first(block, send_by, cut):
    first, second = block[:cut], block[cut:]
    passing = send_by(first, 1), send_by(second, -1)
    return passing, (send_by(second, 1), send_by(first, -1))


def gather_passed(block, passing, rest, send_by):
    far = send_by(passing[0], 1), send_by(passing[1], -1)
    return block, rest[1], passing[1], far[0], far[1], passing[0], rest[0]


def along(axis):
    return lambda x, by: send(x, axis, by)


def turning(turned):
    return lambda x, by: send_turned(x, turned, by)


def in_vmem(kernel, arrays, out_shapes, name):
    moved = sum(a.size * a.dtype.itemsize for a in arrays) + sum(
        o.size * o.dtype.itemsize for o in out_shapes
    )
    return pl.pallas_call(
        kernel,
        out_shape=out_shapes,
        in_specs=[pl.BlockSpec(memory_space=pltpu.VMEM)] * len(arrays),
        out_specs=[pl.BlockSpec(memory_space=pltpu.VMEM)] * len(out_shapes),
        compiler_params=pltpu.CompilerParams(vmem_limit_bytes=2 * moved + 8 * 2**20),
        cost_estimate=pl.CostEstimate(flops=0, bytes_accessed=moved, transcendentals=0),
        name=name,
    )(*arrays)


def ring_places(here):
    return [(here + by) & 3 for by in (0, 1, 2, 2, 3)]


def ring_kernel(index, cut, *refs):
    out = refs[5]
    for at, (place, ref) in enumerate(zip(ring_places(index()), refs[:5])):
        if at == 2:
            out[place, :cut] = ref[...]
        elif at == 3:
            out[place, cut:] = ref[...]
        else:
            out[place] = ref[...]


def ring_parts_kernel(index, cut, *refs):
    out = refs[7]
    here = index()
    out[here] = refs[0][...]
    for by in (1, 2, 3):
        out[(here + by) & 3, :cut] = refs[2 * by - 1][...]
        out[(here + by) & 3, cut:] = refs[2 * by][...]


def ring_order(blocks, index, cut, name):
    shape = jax.ShapeDtypeStruct((4, *blocks[0].shape), blocks[0].dtype)
    kernel = ring_kernel if len(blocks) == 5 else ring_parts_kernel
    return in_vmem(functools.partial(kernel, index, cut), blocks, [shape], name)[0]


def index_along(axis):
    return lambda: lax.axis_index(axis)


def index_turning(turned):
    def index():
        on_z = (lax.axis_index("core") == 0) != turned
        return jnp.where(on_z, lax.axis_index("z"), lax.axis_index("x"))

    return index


def stack_kernel(*refs):
    out = refs[-1]
    start = 0
    for ref in refs[:-1]:
        out[start : start + ref.shape[0]] = ref[...]
        start += ref.shape[0]


def stacked(blocks, name):
    rows = sum(block.shape[0] for block in blocks)
    shape = jax.ShapeDtypeStruct((rows, blocks[0].shape[1]), blocks[0].dtype)
    return in_vmem(stack_kernel, blocks, [shape], name)[0]


def weight_grads_kernel(rows, normed, back, grad_gate_up, active, out):
    wide = grad_gate_up.shape[1]

    @pl.loop(0, normed.shape[1] // rows)
    def _(at):
        part = pl.ds(pl.multiple_of(at * rows, rows), rows)
        left = normed[:, part]
        out[part, :wide] = dot(left, grad_gate_up[...], 0, 0).astype(BF16)
        out[part, wide:] = dot(back[:, part], active[...], 0, 0).astype(BF16)


def chips_kernel(*refs):
    out = refs[5]
    zero = lax.axis_index("core") == 0
    for is_zero in (True, False):

        @pl.when(zero == is_zero)
        def _():
            places = ring_places(lax.axis_index("x" if is_zero else "z"))
            for at, (place, ref) in enumerate(zip(places, refs[:5])):
                cut = {2: slice(0, 2), 3: slice(2, 4)}.get(at, slice(0, 4))
                if is_zero:
                    out[place, cut] = ref[...]
                else:
                    out[cut, place] = ref[...]


def both_kernel(feed, grad, out):
    out[:, 0] = feed[...].reshape(out.shape[0], out.shape[2], out.shape[3])
    out[:, 1] = grad[...].astype(BF16).reshape(out.shape[0], out.shape[2], out.shape[3])


def by_index(pieces, index):
    here = index()
    return lambda by: lax.dynamic_index_in_dim(pieces, (here + by) & 3, 0, keepdims=False)


tie = lax.optimization_barrier


def scatter_far(piece, send_by, along, cut):
    far_first, far_second = halves(piece(2).astype(BF16), along, cut)
    return send_by(far_first, 1), send_by(far_second, -1)


def scatter_near(piece, far, send_by, along, cut):
    from_before, from_after = far
    up_first, up_second = halves(piece(1), along, cut)
    down_first, down_second = halves(piece(3), along, cut)
    upward = jnp.concatenate(
        [(up_first.astype(F32) + from_before.astype(F32)).astype(BF16), up_second.astype(BF16)],
        axis=along,
    )
    downward = jnp.concatenate(
        [down_first.astype(BF16), (down_second.astype(F32) + from_after.astype(F32)).astype(BF16)],
        axis=along,
    )
    return send_by(upward, 1), send_by(downward, -1)


def scatter_first(piece, send_by, along, cut):
    far = scatter_far(piece, send_by, along, cut)
    up = halves(piece(1), along, cut)[1].astype(BF16)
    down = halves(piece(3), along, cut)[0].astype(BF16)
    return far, (send_by(up, 1), send_by(down, -1))


def scatter_passed(piece, far, send_by, along, cut):
    up = halves(piece(1), along, cut)[0].astype(F32) + far[0].astype(F32)
    down = halves(piece(3), along, cut)[1].astype(F32) + far[1].astype(F32)
    return send_by(up.astype(BF16), 1), send_by(down.astype(BF16), -1)


def scatter_joined(piece, passed, rest, along):
    from_before = jnp.concatenate([passed[0], rest[0]], axis=along)
    from_after = jnp.concatenate([rest[1], passed[1]], axis=along)
    return scatter_sum(piece, (from_before, from_after))


def scatter_sum(piece, near):
    return piece(0).astype(F32) + (near[0].astype(F32) + near[1].astype(F32))


def all_sum(x, axis):
    return (x + send(x, axis, 2)) + (send(x, axis, 1) + send(x, axis, -1))


def seq_sum(x):
    x = all_sum(all_sum(x, "x"), "z")
    return x + send(x, "core", 1)


def normalize(values, gain_row):
    inverse = lax.rsqrt(jnp.mean(values * values, axis=1, keepdims=True) + NORM_EPS)
    unit_rows = values * inverse
    return (unit_rows, inverse, unit_rows * gain_row)


def norm_back(upstream, unit_rows, inverse, gain_row):
    scaled = upstream * gain_row
    return inverse * (scaled - unit_rows * jnp.mean(scaled * unit_rows, axis=1, keepdims=True))


def chosen(first, yes, no):
    return jnp.where(first, yes, no)


def in_lanes(columns):
    lane = lax.broadcasted_iota(jnp.int32, (1, LANES), 1)
    return sum(jnp.where(lane == at, column, 0.0) for at, column in enumerate(columns))


def in_rows_of(rows):
    line = lax.broadcasted_iota(jnp.int32, (8, 1), 0)
    return sum(jnp.where(line == at, r, 0.0) for at, r in rows.items())


def total(x):
    return jnp.sum(jnp.sum(x, axis=0, keepdims=True), axis=1, keepdims=True)


def flag(axes):
    first = functools.reduce(jnp.logical_and, [lax.axis_index(axis) == 0 for axis in axes])
    return jnp.where(first, 1.0, 0.0)


def sizes_in_lanes(sizes):
    return in_lanes([jnp.full((1, 1), size, F32) for size in sizes])


def early_kernel(turned, width, first, gate, up, down, conv, lines, crosses, out):
    seq_first, model_first = flag(("x", "z", "core")), flag(("y",))
    split = 3 * width
    weights = [first[:, :split], first[:, split:], gate[...], up[...], down[...]]
    squares = [total(w * w) for w in weights] + [total(conv[...] * conv[...]) * seq_first]
    cross_rows = [crosses[0:1, :split], crosses[0:1, split : split + width]]
    cross_rows += [crosses[at : at + 1, :] for at in (1, 2, 3)]
    moments = [
        total(cross_rows[at]) * seq_first
        if turned[at]
        else total(lines[:, at : at + 1]) * model_first
        for at in range(5)
    ]
    out[...] = in_rows_of({1: in_lanes(squares), 3: in_lanes(moments)})


def squares_kernel(
    half, first_kept, first_given, kept, given, conv, gain, first, gate, up, down, lines, crosses
):
    zero = lax.axis_index("core") == 0
    wide = first_kept.shape[1]
    low = jnp.where(zero, first_kept[...], first_given[...]).astype(F32)
    high = jnp.where(zero, first_given[...], first_kept[...]).astype(F32)
    first[:, :wide] = low
    first[:, wide:] = high
    rest = gate.shape[1] - half
    for at, ref in enumerate((gate, up, down)):
        cols = slice(at * half, (at + 1) * half)
        low = jnp.where(zero, kept[:, cols], given[:, cols]).astype(F32)
        high = jnp.where(zero, given[:, cols], kept[:, cols]).astype(F32)
        ref[:, :half] = low
        ref[:, half:] = high[:, :rest]
    split = 3 * (wide // 2)
    crosses[...] = jnp.zeros_like(crosses)
    sums = []
    parts = [(0, 0, first[:, :split]), (0, split, first[:, split:])]
    parts += [(1, 0, gate[...]), (2, 0, up[...]), (3, 0, down[...])]
    for row, start, grad in parts:
        square = grad * grad + SQUARE_EPS
        sums.append(jnp.sum(square, axis=1, keepdims=True))
        crosses[row : row + 1, start : start + grad.shape[1]] = jnp.sum(
            square, axis=0, keepdims=True
        )
    lines[...] = in_lanes(sums)
    crosses[4:6, : gain.shape[1]] = gain[...]
    width = conv.shape[1]
    for tap in range(KERNEL):
        crosses[6:7, tap * width : (tap + 1) * width] = conv[tap : tap + 1, :]


def moments_kernel(width, cross_full, refs_in, refs_out):
    lines, line_states, crosses, cross_states, early, first, gate, up, down = refs_in
    new_lines, new_crosses, conv_update, u_first, u_gate, u_up, u_down, terms = refs_out
    seq_first, model_first = flag(("x", "z", "core")), flag(("y",))
    line_mean = lines[...] / sizes_in_lanes([*cross_full, *[1.0] * (LANES - 5)][:8])
    lane = lax.broadcasted_iota(jnp.int32, (1, LANES), 1)
    line_mean = jnp.where(lane < 5, line_mean, 0.0)
    fresh = DECAY_RATE * line_states[...] + (1.0 - DECAY_RATE) * line_mean
    new_lines[...] = fresh
    across = DECAY_RATE * cross_states[0:4, :] + (1.0 - DECAY_RATE) * (crosses[0:4, :] / D)
    new_crosses[...] = jnp.zeros_like(new_crosses)
    new_crosses[0:4, :] = across
    conv_grad = crosses[6:7, : KERNEL * width]
    conv_moment = DECAY_RATE * cross_states[6:7, : KERNEL * width] + (1.0 - DECAY_RATE) * (
        conv_grad * conv_grad + SQUARE_EPS
    )
    new_crosses[6:7, : KERNEL * width] = conv_moment
    moved = conv_grad * lax.rsqrt(conv_moment)
    for tap in range(KERNEL):
        conv_update[tap : tap + 1, :] = moved[:, tap * width : (tap + 1) * width]
    split = 3 * width
    sums = []
    for slot, (grad, out, row, cols) in enumerate(
        (
            (first, u_first, 0, slice(0, split)),
            (first, u_first, 0, slice(split, split + width)),
            (gate, u_gate, 1, slice(None)),
            (up, u_up, 2, slice(None)),
            (down, u_down, 3, slice(None)),
        )
    ):
        second = fresh[:, slot : slot + 1] * across[row : row + 1, cols]
        update = grad[:, cols] * lax.rsqrt(second)
        out[:, cols] = update
        sums.append(total(update * update))
    sums.append(total(moved * moved) * seq_first)
    squares = jnp.sum(lines[...], axis=0, keepdims=True) * model_first
    terms[...] = early[...] + in_rows_of({0: in_lanes(sums), 2: squares})


def weights_kernel(width, cross_full, turned, refs_in, refs_out):
    sums, gain_sums, conv, conv_update, gains, gain_moment, *rest = refs_in
    weights, updates = rest[:4], rest[4:]
    conv_new, gains_new, gain_moment_new, gain_grad, *news = refs_out
    rows = [full if turn else D for full, turn in zip(cross_full, turned)]
    cols = [D if turn else full for full, turn in zip(cross_full, turned)]
    lane = lax.broadcasted_iota(jnp.int32, (1, LANES), 1)
    rows_lane = jnp.where(lane < 5, sizes_in_lanes(rows), 1.0)
    cols_lane = jnp.where(lane < 5, sizes_in_lanes(cols), 1.0)
    counts = jnp.where(lane < 5, rows_lane * cols_lane, float(KERNEL * D))
    table = sums[...]
    row_mean = (
        DECAY_RATE * table[3:4] + (1.0 - DECAY_RATE) * (table[2:3] / cols_lane)
    ) / rows_lane
    row_mean = jnp.where(lane < 5, row_mean, 1.0)
    update_rms = jnp.sqrt(row_mean * (table[0:1] / counts))
    weight_rms = jnp.sqrt(table[1:2] / counts)
    factor = STEP_RATE * weight_rms / jnp.maximum(1.0, update_rms / CLIP_LIMIT)
    factor = factor * jnp.sqrt(row_mean)
    split = 3 * width
    for slot, (at, part) in enumerate(
        (
            (0, slice(0, split)),
            (0, slice(split, split + width)),
            (1, slice(None)),
            (2, slice(None)),
            (3, slice(None)),
        )
    ):
        news[at][:, part] = (
            weights[at][:, part] - factor[:, slot : slot + 1] * updates[at][:, part]
        )
    conv_new[...] = conv[...] - factor[:, 5:6] * conv_update[...]
    grad = gain_sums[...]
    gain_grad[...] = grad
    moment = DECAY_RATE * gain_moment[...] + (1.0 - DECAY_RATE) * (grad * grad + SQUARE_EPS)
    gain_moment_new[...] = moment
    update = grad * lax.rsqrt(moment)
    count = float(D)
    update_rms = jnp.sqrt(jnp.sum(update * update, axis=1, keepdims=True) / count)
    weight_rms = jnp.sqrt(jnp.sum(gains[...] * gains[...], axis=1, keepdims=True) / count)
    gains_new[...] = gains[...] - STEP_RATE * weight_rms * (
        update / jnp.maximum(1.0, update_rms / CLIP_LIMIT)
    )


def with_refs(kernel, n_in, *refs):
    kernel(refs[:n_in], refs[n_in:])


def on_device(
    block_input,
    cotangent,
    norm_gains,
    conv_weight,
    in_weight,
    out_weight,
    gate_weight,
    up_weight,
    down_weight,
    in_rows,
    in_cols,
    out_rows,
    out_cols,
    gate_rows,
    gate_cols,
    up_rows,
    up_cols,
    down_rows,
    down_cols,
    conv_moment,
    gain_moment,
):
    rows_here = block_input.shape[0]
    width = conv_weight.shape[1]
    owned = in_weight.shape[0]
    hidden = gate_weight.shape[1]
    halo_rows = KERNEL - 1
    seq_axes = ("x", "z", "core")
    core = lax.axis_index("core")
    model = lax.axis_index("y")
    blocks_per_seq = lax.axis_size(seq_axes) // SEQS
    block_place = lax.axis_index(seq_axes) % blocks_per_seq
    has_before = (block_place != 0).astype(F32)
    has_after = (block_place != blocks_per_seq - 1).astype(F32)
    tokens = rows_here // 4

    in_flat = in_weight.reshape(owned, 3 * width)
    out_turned = out_weight.T
    down_turned = down_weight.T

    zero = core == 0
    chips = ("x", "z")
    pair = 2 * owned

    def both_rows(low, high):
        kept = chosen(zero, low, high)
        given = send(chosen(zero, high, low), "core", 1)
        return jnp.concatenate(
            [chosen(zero, kept, given), chosen(zero, given, kept)], axis=0
        ), given

    in_bf16 = in_flat.astype(BF16)
    first_shard, given = both_rows(
        in_bf16[:, : 2 * width],
        jnp.concatenate([in_bf16[:, 2 * width :], out_turned.astype(BF16)], axis=1),
    )
    part = ring_gather(first_shard, turning(False), owned)

    second, given = tie(((gate_weight, up_weight, down_weight), given))
    padded_hidden = -(-hidden // (2 * LANES)) * 2 * LANES
    half = padded_hidden // 2
    second = [
        jnp.pad(w.astype(BF16), ((0, 0), (0, padded_hidden - hidden)))
        for w in (second[0], second[1], second[2].T)
    ]
    second_shard, _ = both_rows(
        jnp.concatenate([w[:, :half] for w in second], axis=1),
        jnp.concatenate([w[:, half:] for w in second], axis=1),
    )

    part = ring_order(part, index_turning(False), owned, "order_first")
    unit_one, inverse_one, normed_value = normalize(block_input, norm_gains[0])
    near, second_shard = tie((gather_near(part, turning(True)), second_shard))
    second_matrix = lax.all_gather(second_shard, chips, axis=0, tiled=True)
    gate_matrix = second_matrix[:, :half]
    up_matrix = second_matrix[:, half : 2 * half]
    gate_up_matrix = second_matrix[:, : 2 * half]
    down_matrix = second_matrix[:, 2 * half :]
    (first_kept,) = in_vmem(
        chips_kernel,
        gather_far(part, near, turning(True), 2),
        [jax.ShapeDtypeStruct((4, 4, pair, 2 * width), BF16)],
        "order_chips",
    )
    first_kept = first_kept.reshape(D, 2 * width)
    first_given = send(first_kept, "core", 1)
    out_matrix = chosen(zero, first_given[:, width:], first_kept[:, width:])

    def own_tokens(x):
        return lax.dynamic_slice_in_dim(x, model * tokens, tokens, axis=0)

    def piece_of(x):
        return by_index(x.reshape(4, tokens, D), index_along("y"))

    def both_cores(x):
        return stacked([x, send(x, "core", 1)], "both_cores")

    def core_scatter(partial):
        other = send(partial[rows_here:].astype(BF16), "core", 1)
        return partial[:rows_here] + other.astype(F32)

    normed = normed_value.astype(BF16)
    projected_kept = dot(normed, first_kept, 1, 0)
    projected_given = dot(normed, first_given, 1, 0)
    b_part = chosen(zero, projected_kept[:, :width], projected_given[:, :width])
    c_part = chosen(zero, projected_kept[:, width:], projected_given[:, width:])
    x_part = chosen(zero, projected_given[:, :width], projected_kept[:, :width])
    product = b_part * x_part
    earlier = shifted(product[rows_here - halo_rows :], seq_axes, 1) * has_before
    padded = jnp.concatenate([earlier, product], axis=0)
    convolved = conv_weight[0] * padded[0:rows_here]
    for offset in range(1, KERNEL):
        convolved = convolved + conv_weight[offset] * padded[offset : offset + rows_here]
    gated = (c_part * convolved).astype(BF16)
    branch = dot(gated, out_matrix, 1, 1)
    branch, cotangent_late = tie((branch.astype(BF16), cotangent))
    back_feed = both_cores(cotangent_late.astype(BF16))
    branch, back_feed = tie((exchange(branch.reshape(4, tokens, D), "y"), back_feed))
    middle = own_tokens(block_input) + jnp.sum(branch.astype(F32), axis=0)
    unit_two, inverse_two, normed_value_two = normalize(middle, norm_gains[1])
    grad_active = dot(back_feed, down_matrix, 1, 0)
    normed_two = normed_value_two.astype(BF16)
    passing, rest = gather_first(normed_two, along("y"), tokens // 2)
    blocks = gather_passed(normed_two, passing, rest, along("y"))
    blocks, grad_active = tie((blocks, grad_active))
    normed_two = ring_order(
        blocks,
        index_along("y"),
        tokens // 2,
        "order_tokens",
    )
    normed_two = both_cores(normed_two.reshape(rows_here, D))
    gate_pre = dot(normed_two, gate_matrix, 1, 0)
    upward = dot(normed_two, up_matrix, 1, 0)
    sigmoid_gate = jax.nn.sigmoid(gate_pre)
    silu_gate = gate_pre * sigmoid_gate
    active = (silu_gate * upward).astype(BF16)

    grad_gate = (
        grad_active * upward * (sigmoid_gate * (1.0 + gate_pre * (1.0 - sigmoid_gate)))
    ).astype(BF16)
    grad_upward = (grad_active * silu_gate).astype(BF16)
    grad_gate_up = jnp.concatenate([grad_gate, grad_upward], axis=1)
    partial = dot(grad_gate_up, gate_up_matrix, 1, 1)
    other, active, grad_gate_up = tie(
        (send(partial[rows_here:].astype(BF16), "core", 1), active, grad_gate_up)
    )
    normed_sums = (partial[:rows_here] + other.astype(F32)).astype(BF16)
    (second_full,) = in_vmem(
        functools.partial(weight_grads_kernel, 2 * LANES),
        [normed_two, back_feed, grad_gate_up, active],
        [jax.ShapeDtypeStruct((D, 3 * half), BF16)],
        "weight_grads",
    )
    normed_sums, second_full = tie(
        (exchange(normed_sums.reshape(4, tokens, D), "y"), second_full)
    )
    feed_partial = dot(active, down_matrix, 1, 1)
    normed_sums, feed_partial = tie((normed_sums, feed_partial))
    second_sum = lax.psum_scatter(second_full, chips, scatter_dimension=0, tiled=True)
    grad_normed_two = jnp.sum(normed_sums.astype(F32), axis=0)
    grad_middle = own_tokens(cotangent) + norm_back(
        grad_normed_two, unit_two, inverse_two, norm_gains[1]
    )
    back_branch = grad_middle.astype(BF16)
    feed_here = core_scatter(feed_partial)
    passing, rest = gather_first(back_branch, along("y"), tokens // 2)
    blocks = gather_passed(back_branch, passing, rest, along("y"))
    blocks, feed_here = tie((blocks, feed_here.astype(BF16)))
    back_branch = ring_order(
        blocks, index_along("y"), tokens // 2, "order_back"
    ).reshape(rows_here, D)

    def own_rows(summed):
        kept = chosen(zero, summed[:owned], summed[owned:])
        return kept, send(chosen(zero, summed[owned:], summed[:owned]), "core", 1)

    second_kept, second_given = own_rows(second_sum)

    out_grad_full = dot(back_branch, gated, 0, 0).astype(BF16)
    grad_gated = dot(back_branch, out_matrix, 1, 0)
    grad_c = grad_gated * convolved
    grad_conv = grad_gated * c_part
    later = shifted(grad_conv[:halo_rows], seq_axes, -1) * has_after
    extended = jnp.concatenate([grad_conv, later], axis=0)
    grad_product = conv_weight[0] * extended[halo_rows : halo_rows + rows_here]
    for offset in range(1, KERNEL):
        grad_product = (
            grad_product
            + conv_weight[offset] * extended[halo_rows - offset : halo_rows - offset + rows_here]
        )
    conv_part = jnp.concatenate(
        [
            jnp.sum(grad_conv * padded[offset : offset + rows_here], axis=0, keepdims=True)
            for offset in range(KERNEL)
        ]
    )
    grad_low = jnp.concatenate([grad_product * x_part, grad_c], axis=1).astype(BF16)
    grad_high = (grad_product * b_part).astype(BF16)
    first_grad_low = dot(normed, grad_low, 0, 0).astype(BF16)
    first_grad_high = jnp.concatenate(
        [dot(normed, grad_high, 0, 0).astype(BF16), out_grad_full], axis=1
    )
    first_other = send(chosen(zero, first_grad_high, first_grad_low), "core", 1)

    wide_high = jnp.concatenate([grad_high, jnp.zeros_like(grad_high)], axis=1)
    grad_normed_here = dot(chosen(zero, grad_low, wide_high), first_kept, 1, 1) + dot(
        chosen(zero, wide_high, grad_low), first_given, 1, 1
    )
    (both,) = in_vmem(
        both_kernel,
        [feed_here, grad_normed_here],
        [jax.ShapeDtypeStruct((4, 2, tokens, D), BF16)],
        "both_pieces",
    )
    first_other, both = tie((first_other, both))
    both = exchange(both, "y")
    first_sum = chosen(zero, first_grad_low, first_grad_high).astype(F32) + first_other.astype(F32)
    first_sum = first_sum.astype(BF16).reshape(4, 4, pair, 2 * width)
    first_sum = chosen(zero, first_sum, jnp.swapaxes(first_sum, 0, 1))
    piece = by_index(first_sum, index_turning(True))
    far, rest = scatter_first(piece, turning(True), 0, 2)
    far, grad_normed_here, grad_normed_two, in_rows, in_cols, late = tie(
        (
            far,
            grad_normed_here,
            grad_normed_two,
            in_rows,
            in_cols,
            (gate_weight, up_weight, down_weight, in_weight, out_weight),
        )
    )

    turned = (False, True, False, False, True)
    cross_full = (3 * D, D, FF, FF, FF)

    def row(x):
        x = x.reshape(1, -1) if x.ndim == 1 else x
        return jnp.pad(x, ((0, 0), (0, hidden - x.shape[1])))

    line_states = in_lanes(
        [state[:, None] for state in (in_rows, out_cols, gate_rows, up_rows, down_cols)]
    )
    cross_states = jnp.concatenate(
        [
            row(jnp.concatenate([in_cols.reshape(3 * width), out_rows])),
            row(gate_cols),
            row(up_cols),
            row(down_rows),
            jnp.zeros((2, hidden), F32),
            row(conv_moment.reshape(KERNEL * width)),
            jnp.zeros((1, hidden), F32),
        ],
        axis=0,
    )
    first_weight = jnp.concatenate([late[3].reshape(owned, 3 * width), late[4].T], axis=1)
    (early,) = in_vmem(
        functools.partial(early_kernel, turned, width),
        [first_weight, late[0], late[1], late[2].T, conv_weight, line_states, cross_states],
        [jax.ShapeDtypeStruct((8, LANES), F32)],
        "early_sums",
    )

    gain_part = jnp.concatenate(
        [
            jnp.sum(grad_normed_here * unit_one, axis=0, keepdims=True),
            jnp.sum(grad_normed_two * unit_two, axis=0, keepdims=True),
        ]
    )
    passed, gain_part = tie((scatter_passed(piece, far, turning(True), 0, 2), gain_part))
    piece = by_index(scatter_joined(piece, passed, rest, 0), index_turning(False))
    far = scatter_far(piece, turning(False), 0, owned)
    far, both = tie((far, both))
    both = jnp.sum(both.astype(F32), axis=0)
    result_here = middle + both[0]
    grad_normed = both[1]
    input_grad_here = grad_middle + norm_back(
        grad_normed, own_tokens(unit_one), own_tokens(inverse_one), norm_gains[0]
    )
    both_here = jnp.concatenate([result_here, input_grad_here], axis=1).astype(BF16)
    near = scatter_near(piece, far, turning(False), 0, owned)
    near, both_here = tie((near, both_here))
    both_full = lax.all_gather(both_here, "y", axis=0, tiled=True)
    first_own, first_other = own_rows(scatter_sum(piece, near).astype(BF16))

    def f32(*shape):
        return jax.ShapeDtypeStruct(shape, F32)

    first_grad, gate_grad, up_grad, down_grad, lines, crosses = in_vmem(
        functools.partial(squares_kernel, half),
        [first_own, first_other, second_kept, second_given, conv_part, gain_part],
        [f32(owned, 4 * width)] + [f32(owned, hidden)] * 3 + [f32(owned, LANES), f32(8, hidden)],
        "square_sums",
    )
    crosses = all_sum(crosses, "x")
    crosses = all_sum(crosses, "z")
    crosses = crosses + send(crosses, "core", 1)
    lines = all_sum(lines, "y")
    conv_grad = crosses[6, : KERNEL * width].reshape(KERNEL, width)
    gain_sums = all_sum(crosses[4:6, :D], "y")
    line_new, cross_new, conv_update, *updates, terms = in_vmem(
        functools.partial(
            with_refs, functools.partial(moments_kernel, width, cross_full), 9
        ),
        [lines, line_states, crosses, cross_states, early, first_grad, gate_grad, up_grad]
        + [down_grad],
        [f32(owned, LANES), f32(8, hidden), f32(KERNEL, width), f32(owned, 4 * width)]
        + [f32(owned, hidden)] * 3
        + [f32(8, LANES)],
        "moments",
    )
    every = ("x", "z", "core", "y")
    terms, both_full = tie((terms, both_full))
    sums = spread(terms[:4].reshape(4 * LANES), every)
    result = both_full[:, :D].astype(F32)
    input_grad = both_full[:, D:].astype(F32)
    gain_sums, sums = tie((gain_sums, sums))
    sums = jnp.sum(sums, axis=0).reshape(4, LANES)
    conv_new, gain_new, gain_moment_new, gain_grad, *news = in_vmem(
        functools.partial(
            with_refs, functools.partial(weights_kernel, width, cross_full, turned), 14
        ),
        [sums, gain_sums, conv_weight, conv_update, norm_gains, gain_moment]
        + [first_weight, late[0], late[1], late[2].T, *updates],
        [f32(KERNEL, width), f32(2, D), f32(2, D), f32(2, D), f32(owned, 4 * width)]
        + [f32(owned, hidden)] * 3,
        "new_weights",
    )
    in_grad, out_grad = first_grad[:, : 3 * width], first_grad[:, 3 * width :]
    in_new, out_new = news[0][:, : 3 * width], news[0][:, 3 * width :]
    in_cols_new = cross_new[0, : 3 * width]
    out_rows_new = cross_new[0, 3 * width : 4 * width]
    conv_moment_new = cross_new[6, : KERNEL * width].reshape(KERNEL, width)
    return (
        result,
        input_grad,
        in_grad.reshape(in_weight.shape),
        out_grad.T,
        gate_grad,
        up_grad,
        down_grad.T,
        conv_grad,
        gain_grad,
        in_new.reshape(in_weight.shape),
        out_new.T,
        news[1],
        news[2],
        news[3].T,
        conv_new,
        gain_new,
        line_new[:, 0],
        in_cols_new.reshape(in_cols.shape),
        out_rows_new,
        line_new[:, 1],
        line_new[:, 2],
        cross_new[1],
        line_new[:, 3],
        cross_new[2],
        cross_new[3],
        line_new[:, 4],
        conv_moment_new,
        gain_moment_new,
    )


def solution(mesh):
    seq = ("x", "z", "core")
    model = "y"
    inner = Mesh(mesh.devices.reshape(4, 4, 2, 4), ("x", "z", "core", "y"))
    in_specs = (
        P(seq, None),
        P(seq, None),
        P(),
        P(None, model),
        P(seq, None, model),
        P(model, seq),
        P(seq, model),
        P(seq, model),
        P(model, seq),
        P(seq),
        P(None, model),
        P(model),
        P(seq),
        P(seq),
        P(model),
        P(seq),
        P(model),
        P(model),
        P(seq),
        P(None, model),
        P(),
    )
    out_specs = (
        P(seq, None),
        P(seq, None),
        P(seq, None, model),
        P(model, seq),
        P(seq, model),
        P(seq, model),
        P(model, seq),
        P(None, model),
        P(),
        P(seq, None, model),
        P(model, seq),
        P(seq, model),
        P(seq, model),
        P(model, seq),
        P(None, model),
        P(),
        P(seq),
        P(None, model),
        P(model),
        P(seq),
        P(seq),
        P(model),
        P(seq),
        P(model),
        P(model),
        P(seq),
        P(None, model),
        P(),
    )
    return jax.shard_map(
        on_device, mesh=inner, in_specs=in_specs, out_specs=out_specs, check_vma=False
    )
```

```python
import functools

import jax
import jax.numpy as jnp
from jax import lax
from jax.experimental import pallas as pl
from jax.experimental.pallas import tpu as pltpu
from jax.sharding import Mesh
from jax.sharding import PartitionSpec as P

D = 1536
FF = 6912
KERNEL = 3
SEQS = 2

NORM_EPS = 1e-05
DECAY_RATE = 0.5
SQUARE_EPS = 1e-30
CLIP_LIMIT = 0.2
STEP_RATE = 4.0

BF16 = jnp.bfloat16
F32 = jnp.float32
LANES = 128


def send(x, axis, by):
    size = lax.axis_size(axis)
    return lax.ppermute(x, axis, [(i, (i + by) % size) for i in range(size)])


def shifted(x, axis, by):
    size = lax.axis_size(axis)
    pairs = [(i, i + by) for i in range(size) if 0 <= i + by < size]
    return lax.ppermute(x, axis, pairs)


def dot(left_side, right_side, left_axis, right_axis):
    return lax.dot_general(
        left_side,
        right_side,
        (((left_axis,), (right_axis,)), ((), ())),
        preferred_element_type=F32,
    )


def exchange(x, axes):
    return lax.all_to_all(x, axes, split_axis=0, concat_axis=0, tiled=True)


def spread(x, axes):
    return exchange(jnp.broadcast_to(x, (lax.axis_size(axes), *x.shape)), axes)


def halves(x, axis, cut):
    size = x.shape[axis]
    return (
        lax.slice_in_dim(x, 0, cut, axis=axis),
        lax.slice_in_dim(x, cut, size, axis=axis),
    )


def send_turned(x, turned, by):
    pairs = []
    for i in range(32):
        at = [i // 8, i // 2 % 4]
        axis = (1 - i % 2) ^ turned
        at[axis] = (at[axis] + by) % 4
        pairs.append((i, at[0] * 8 + at[1] * 2 + i % 2))
    return lax.ppermute(x, ("x", "z", "core"), pairs)


def gather_near(block, send_by):
    return send_by(block, 1), send_by(block, -1)


def gather_far(block, near, send_by, cut):
    before, after = near
    return block, after, send_by(before[:cut], 1), send_by(after[cut:], -1), before


def ring_gather(block, send_by, cut):
    return gather_far(block, gather_near(block, send_by), send_by, cut)


def gather_first(block, send_by, cut):
    first, second = block[:cut], block[cut:]
    passing = send_by(first, 1), send_by(second, -1)
    return passing, (send_by(second, 1), send_by(first, -1))


def gather_passed(block, passing, rest, send_by):
    far = send_by(passing[0], 1), send_by(passing[1], -1)
    return block, rest[1], passing[1], far[0], far[1], passing[0], rest[0]


def along(axis):
    return lambda x, by: send(x, axis, by)


def turning(turned):
    return lambda x, by: send_turned(x, turned, by)


def in_vmem(kernel, arrays, out_shapes, name):
    moved = sum(a.size * a.dtype.itemsize for a in arrays) + sum(
        o.size * o.dtype.itemsize for o in out_shapes
    )
    return pl.pallas_call(
        kernel,
        out_shape=out_shapes,
        in_specs=[pl.BlockSpec(memory_space=pltpu.VMEM)] * len(arrays),
        out_specs=[pl.BlockSpec(memory_space=pltpu.VMEM)] * len(out_shapes),
        compiler_params=pltpu.CompilerParams(vmem_limit_bytes=2 * moved + 8 * 2**20),
        cost_estimate=pl.CostEstimate(flops=0, bytes_accessed=moved, transcendentals=0),
        name=name,
    )(*arrays)


def ring_places(here):
    return [(here + by) & 3 for by in (0, 1, 2, 2, 3)]


def ring_kernel(index, cut, *refs):
    out = refs[5]
    for at, (place, ref) in enumerate(zip(ring_places(index()), refs[:5])):
        if at == 2:
            out[place, :cut] = ref[...]
        elif at == 3:
            out[place, cut:] = ref[...]
        else:
            out[place] = ref[...]


def ring_parts_kernel(index, cut, *refs):
    out = refs[7]
    here = index()
    out[here] = refs[0][...]
    for by in (1, 2, 3):
        out[(here + by) & 3, :cut] = refs[2 * by - 1][...]
        out[(here + by) & 3, cut:] = refs[2 * by][...]


def ring_order(blocks, index, cut, name):
    shape = jax.ShapeDtypeStruct((4, *blocks[0].shape), blocks[0].dtype)
    kernel = ring_kernel if len(blocks) == 5 else ring_parts_kernel
    return in_vmem(functools.partial(kernel, index, cut), blocks, [shape], name)[0]


def index_along(axis):
    return lambda: lax.axis_index(axis)


def index_turning(turned):
    def index():
        on_z = (lax.axis_index("core") == 0) != turned
        return jnp.where(on_z, lax.axis_index("z"), lax.axis_index("x"))

    return index


def stack_kernel(*refs):
    out = refs[-1]
    start = 0
    for ref in refs[:-1]:
        out[start : start + ref.shape[0]] = ref[...]
        start += ref.shape[0]


def stacked(blocks, name):
    rows = sum(block.shape[0] for block in blocks)
    shape = jax.ShapeDtypeStruct((rows, blocks[0].shape[1]), blocks[0].dtype)
    return in_vmem(stack_kernel, blocks, [shape], name)[0]


def weight_grads_kernel(rows, normed, back, grad_gate_up, active, out):
    wide = grad_gate_up.shape[1]

    @pl.loop(0, normed.shape[1] // rows)
    def _(at):
        part = pl.ds(pl.multiple_of(at * rows, rows), rows)
        left = normed[:, part]
        out[part, :wide] = dot(left, grad_gate_up[...], 0, 0).astype(BF16)
        out[part, wide:] = dot(back[:, part], active[...], 0, 0).astype(BF16)


def chips_kernel(*refs):
    out = refs[5]
    zero = lax.axis_index("core") == 0
    for is_zero in (True, False):

        @pl.when(zero == is_zero)
        def _():
            places = ring_places(lax.axis_index("x" if is_zero else "z"))
            for at, (place, ref) in enumerate(zip(places, refs[:5])):
                cut = {2: slice(0, 2), 3: slice(2, 4)}.get(at, slice(0, 4))
                if is_zero:
                    out[place, cut] = ref[...]
                else:
                    out[cut, place] = ref[...]


def both_kernel(feed, grad, out):
    out[:, 0] = feed[...].reshape(out.shape[0], out.shape[2], out.shape[3])
    out[:, 1] = grad[...].astype(BF16).reshape(out.shape[0], out.shape[2], out.shape[3])


def by_index(pieces, index):
    here = index()
    return lambda by: lax.dynamic_index_in_dim(pieces, (here + by) & 3, 0, keepdims=False)


tie = lax.optimization_barrier


def scatter_far(piece, send_by, along, cut):
    far_first, far_second = halves(piece(2).astype(BF16), along, cut)
    return send_by(far_first, 1), send_by(far_second, -1)


def scatter_near(piece, far, send_by, along, cut):
    from_before, from_after = far
    up_first, up_second = halves(piece(1), along, cut)
    down_first, down_second = halves(piece(3), along, cut)
    upward = jnp.concatenate(
        [(up_first.astype(F32) + from_before.astype(F32)).astype(BF16), up_second.astype(BF16)],
        axis=along,
    )
    downward = jnp.concatenate(
        [down_first.astype(BF16), (down_second.astype(F32) + from_after.astype(F32)).astype(BF16)],
        axis=along,
    )
    return send_by(upward, 1), send_by(downward, -1)


def scatter_first(piece, send_by, along, cut):
    far = scatter_far(piece, send_by, along, cut)
    up = halves(piece(1), along, cut)[1].astype(BF16)
    down = halves(piece(3), along, cut)[0].astype(BF16)
    return far, (send_by(up, 1), send_by(down, -1))


def scatter_passed(piece, far, send_by, along, cut):
    up = halves(piece(1), along, cut)[0].astype(F32) + far[0].astype(F32)
    down = halves(piece(3), along, cut)[1].astype(F32) + far[1].astype(F32)
    return send_by(up.astype(BF16), 1), send_by(down.astype(BF16), -1)


def scatter_joined(piece, passed, rest, along):
    from_before = jnp.concatenate([passed[0], rest[0]], axis=along)
    from_after = jnp.concatenate([rest[1], passed[1]], axis=along)
    return scatter_sum(piece, (from_before, from_after))


def scatter_sum(piece, near):
    return piece(0).astype(F32) + (near[0].astype(F32) + near[1].astype(F32))


def all_sum(x, axis):
    return (x + send(x, axis, 2)) + (send(x, axis, 1) + send(x, axis, -1))


def seq_sum(x):
    x = all_sum(all_sum(x, "x"), "z")
    return x + send(x, "core", 1)


def normalize(values, gain_row):
    inverse = lax.rsqrt(jnp.mean(values * values, axis=1, keepdims=True) + NORM_EPS)
    unit_rows = values * inverse
    return (unit_rows, inverse, unit_rows * gain_row)


def norm_back(upstream, unit_rows, inverse, gain_row):
    scaled = upstream * gain_row
    return inverse * (scaled - unit_rows * jnp.mean(scaled * unit_rows, axis=1, keepdims=True))


def chosen(first, yes, no):
    return jnp.where(first, yes, no)


def in_lanes(columns):
    lane = lax.broadcasted_iota(jnp.int32, (1, LANES), 1)
    return sum(jnp.where(lane == at, column, 0.0) for at, column in enumerate(columns))


def in_rows_of(rows):
    line = lax.broadcasted_iota(jnp.int32, (8, 1), 0)
    return sum(jnp.where(line == at, r, 0.0) for at, r in rows.items())


def total(x):
    return jnp.sum(jnp.sum(x, axis=0, keepdims=True), axis=1, keepdims=True)


def flag(axes):
    first = functools.reduce(jnp.logical_and, [lax.axis_index(axis) == 0 for axis in axes])
    return jnp.where(first, 1.0, 0.0)


def sizes_in_lanes(sizes):
    return in_lanes([jnp.full((1, 1), size, F32) for size in sizes])


def early_kernel(turned, width, first, gate, up, down, conv, lines, crosses, out):
    seq_first, model_first = flag(("x", "z", "core")), flag(("y",))
    split = 3 * width
    weights = [first[:, :split], first[:, split:], gate[...], up[...], down[...]]
    squares = [total(w * w) for w in weights] + [total(conv[...] * conv[...]) * seq_first]
    cross_rows = [crosses[0:1, :split], crosses[0:1, split : split + width]]
    cross_rows += [crosses[at : at + 1, :] for at in (1, 2, 3)]
    moments = [
        total(cross_rows[at]) * seq_first
        if turned[at]
        else total(lines[:, at : at + 1]) * model_first
        for at in range(5)
    ]
    out[...] = in_rows_of({1: in_lanes(squares), 3: in_lanes(moments)})


def squares_kernel(
    half, first_kept, first_given, kept, given, conv, gain, first, gate, up, down, lines, crosses
):
    zero = lax.axis_index("core") == 0
    wide = first_kept.shape[1]
    low = jnp.where(zero, first_kept[...], first_given[...]).astype(F32)
    high = jnp.where(zero, first_given[...], first_kept[...]).astype(F32)
    first[:, :wide] = low
    first[:, wide:] = high
    rest = gate.shape[1] - half
    for at, ref in enumerate((gate, up, down)):
        cols = slice(at * half, (at + 1) * half)
        low = jnp.where(zero, kept[:, cols], given[:, cols]).astype(F32)
        high = jnp.where(zero, given[:, cols], kept[:, cols]).astype(F32)
        ref[:, :half] = low
        ref[:, half:] = high[:, :rest]
    split = 3 * (wide // 2)
    crosses[...] = jnp.zeros_like(crosses)
    sums = []
    parts = [(0, 0, first[:, :split]), (0, split, first[:, split:])]
    parts += [(1, 0, gate[...]), (2, 0, up[...]), (3, 0, down[...])]
    for row, start, grad in parts:
        square = grad * grad + SQUARE_EPS
        sums.append(jnp.sum(square, axis=1, keepdims=True))
        crosses[row : row + 1, start : start + grad.shape[1]] = jnp.sum(
            square, axis=0, keepdims=True
        )
    lines[...] = in_lanes(sums)
    crosses[4:6, : gain.shape[1]] = gain[...]
    width = conv.shape[1]
    for tap in range(KERNEL):
        crosses[6:7, tap * width : (tap + 1) * width] = conv[tap : tap + 1, :]


def moments_kernel(width, cross_full, refs_in, refs_out):
    lines, line_states, crosses, cross_states, early, first, gate, up, down = refs_in
    new_lines, new_crosses, conv_update, u_first, u_gate, u_up, u_down, terms = refs_out
    seq_first, model_first = flag(("x", "z", "core")), flag(("y",))
    line_mean = lines[...] / sizes_in_lanes([*cross_full, *[1.0] * (LANES - 5)][:8])
    lane = lax.broadcasted_iota(jnp.int32, (1, LANES), 1)
    line_mean = jnp.where(lane < 5, line_mean, 0.0)
    fresh = DECAY_RATE * line_states[...] + (1.0 - DECAY_RATE) * line_mean
    new_lines[...] = fresh
    across = DECAY_RATE * cross_states[0:4, :] + (1.0 - DECAY_RATE) * (crosses[0:4, :] / D)
    new_crosses[...] = jnp.zeros_like(new_crosses)
    new_crosses[0:4, :] = across
    conv_grad = crosses[6:7, : KERNEL * width]
    conv_moment = DECAY_RATE * cross_states[6:7, : KERNEL * width] + (1.0 - DECAY_RATE) * (
        conv_grad * conv_grad + SQUARE_EPS
    )
    new_crosses[6:7, : KERNEL * width] = conv_moment
    moved = conv_grad * lax.rsqrt(conv_moment)
    for tap in range(KERNEL):
        conv_update[tap : tap + 1, :] = moved[:, tap * width : (tap + 1) * width]
    split = 3 * width
    sums = []
    for slot, (grad, out, row, cols) in enumerate(
        (
            (first, u_first, 0, slice(0, split)),
            (first, u_first, 0, slice(split, split + width)),
            (gate, u_gate, 1, slice(None)),
            (up, u_up, 2, slice(None)),
            (down, u_down, 3, slice(None)),
        )
    ):
        second = fresh[:, slot : slot + 1] * across[row : row + 1, cols]
        update = grad[:, cols] * lax.rsqrt(second)
        out[:, cols] = update
        sums.append(total(update * update))
    sums.append(total(moved * moved) * seq_first)
    squares = jnp.sum(lines[...], axis=0, keepdims=True) * model_first
    terms[...] = early[...] + in_rows_of({0: in_lanes(sums), 2: squares})


def weights_kernel(width, cross_full, turned, refs_in, refs_out):
    sums, gain_sums, conv, conv_update, gains, gain_moment, *rest = refs_in
    weights, updates = rest[:4], rest[4:]
    conv_new, gains_new, gain_moment_new, gain_grad, *news = refs_out
    rows = [full if turn else D for full, turn in zip(cross_full, turned)]
    cols = [D if turn else full for full, turn in zip(cross_full, turned)]
    lane = lax.broadcasted_iota(jnp.int32, (1, LANES), 1)
    rows_lane = jnp.where(lane < 5, sizes_in_lanes(rows), 1.0)
    cols_lane = jnp.where(lane < 5, sizes_in_lanes(cols), 1.0)
    counts = jnp.where(lane < 5, rows_lane * cols_lane, float(KERNEL * D))
    table = sums[...]
    row_mean = (
        DECAY_RATE * table[3:4] + (1.0 - DECAY_RATE) * (table[2:3] / cols_lane)
    ) / rows_lane
    row_mean = jnp.where(lane < 5, row_mean, 1.0)
    update_rms = jnp.sqrt(row_mean * (table[0:1] / counts))
    weight_rms = jnp.sqrt(table[1:2] / counts)
    factor = STEP_RATE * weight_rms / jnp.maximum(1.0, update_rms / CLIP_LIMIT)
    factor = factor * jnp.sqrt(row_mean)
    split = 3 * width
    for slot, (at, part) in enumerate(
        (
            (0, slice(0, split)),
            (0, slice(split, split + width)),
            (1, slice(None)),
            (2, slice(None)),
            (3, slice(None)),
        )
    ):
        news[at][:, part] = (
            weights[at][:, part] - factor[:, slot : slot + 1] * updates[at][:, part]
        )
    conv_new[...] = conv[...] - factor[:, 5:6] * conv_update[...]
    grad = gain_sums[...]
    gain_grad[...] = grad
    moment = DECAY_RATE * gain_moment[...] + (1.0 - DECAY_RATE) * (grad * grad + SQUARE_EPS)
    gain_moment_new[...] = moment
    update = grad * lax.rsqrt(moment)
    count = float(D)
    update_rms = jnp.sqrt(jnp.sum(update * update, axis=1, keepdims=True) / count)
    weight_rms = jnp.sqrt(jnp.sum(gains[...] * gains[...], axis=1, keepdims=True) / count)
    gains_new[...] = gains[...] - STEP_RATE * weight_rms * (
        update / jnp.maximum(1.0, update_rms / CLIP_LIMIT)
    )


def with_refs(kernel, n_in, *refs):
    kernel(refs[:n_in], refs[n_in:])


def on_device(
    block_input,
    cotangent,
    norm_gains,
    conv_weight,
    in_weight,
    out_weight,
    gate_weight,
    up_weight,
    down_weight,
    in_rows,
    in_cols,
    out_rows,
    out_cols,
    gate_rows,
    gate_cols,
    up_rows,
    up_cols,
    down_rows,
    down_cols,
    conv_moment,
    gain_moment,
):
    rows_here = block_input.shape[0]
    width = conv_weight.shape[1]
    owned = in_weight.shape[0]
    hidden = gate_weight.shape[1]
    halo_rows = KERNEL - 1
    seq_axes = ("x", "z", "core")
    core = lax.axis_index("core")
    model = lax.axis_index("y")
    blocks_per_seq = lax.axis_size(seq_axes) // SEQS
    block_place = lax.axis_index(seq_axes) % blocks_per_seq
    has_before = (block_place != 0).astype(F32)
    has_after = (block_place != blocks_per_seq - 1).astype(F32)
    tokens = rows_here // 4

    in_flat = in_weight.reshape(owned, 3 * width)
    out_turned = out_weight.T
    down_turned = down_weight.T

    zero = core == 0
    chips = ("x", "z")
    pair = 2 * owned

    def both_rows(low, high):
        kept = chosen(zero, low, high)
        given = send(chosen(zero, high, low), "core", 1)
        return jnp.concatenate(
            [chosen(zero, kept, given), chosen(zero, given, kept)], axis=0
        ), given

    in_bf16 = in_flat.astype(BF16)
    first_shard, given = both_rows(
        in_bf16[:, : 2 * width],
        jnp.concatenate([in_bf16[:, 2 * width :], out_turned.astype(BF16)], axis=1),
    )
    part = ring_gather(first_shard, turning(False), owned)

    second, given = tie(((gate_weight, up_weight, down_weight), given))
    padded_hidden = -(-hidden // (2 * LANES)) * 2 * LANES
    half = padded_hidden // 2
    second = [
        jnp.pad(w.astype(BF16), ((0, 0), (0, padded_hidden - hidden)))
        for w in (second[0], second[1], second[2].T)
    ]
    second_shard, _ = both_rows(
        jnp.concatenate([w[:, :half] for w in second], axis=1),
        jnp.concatenate([w[:, half:] for w in second], axis=1),
    )

    part = ring_order(part, index_turning(False), owned, "order_first")
    unit_one, inverse_one, normed_value = normalize(block_input, norm_gains[0])
    near, second_shard = tie((gather_near(part, turning(True)), second_shard))
    second_matrix = lax.all_gather(second_shard, chips, axis=0, tiled=True)
    gate_matrix = second_matrix[:, :half]
    up_matrix = second_matrix[:, half : 2 * half]
    gate_up_matrix = second_matrix[:, : 2 * half]
    down_matrix = second_matrix[:, 2 * half :]
    (first_kept,) = in_vmem(
        chips_kernel,
        gather_far(part, near, turning(True), 2),
        [jax.ShapeDtypeStruct((4, 4, pair, 2 * width), BF16)],
        "order_chips",
    )
    first_kept = first_kept.reshape(D, 2 * width)
    first_given = send(first_kept, "core", 1)
    out_matrix = chosen(zero, first_given[:, width:], first_kept[:, width:])

    def own_tokens(x):
        return lax.dynamic_slice_in_dim(x, model * tokens, tokens, axis=0)

    def piece_of(x):
        return by_index(x.reshape(4, tokens, D), index_along("y"))

    def both_cores(x):
        return stacked([x, send(x, "core", 1)], "both_cores")

    def core_scatter(partial):
        other = send(partial[rows_here:].astype(BF16), "core", 1)
        return partial[:rows_here] + other.astype(F32)

    normed = normed_value.astype(BF16)
    projected_kept = dot(normed, first_kept, 1, 0)
    projected_given = dot(normed, first_given, 1, 0)
    b_part = chosen(zero, projected_kept[:, :width], projected_given[:, :width])
    c_part = chosen(zero, projected_kept[:, width:], projected_given[:, width:])
    x_part = chosen(zero, projected_given[:, :width], projected_kept[:, :width])
    product = b_part * x_part
    earlier = shifted(product[rows_here - halo_rows :], seq_axes, 1) * has_before
    padded = jnp.concatenate([earlier, product], axis=0)
    convolved = conv_weight[0] * padded[0:rows_here]
    for offset in range(1, KERNEL):
        convolved = convolved + conv_weight[offset] * padded[offset : offset + rows_here]
    gated = (c_part * convolved).astype(BF16)
    branch = dot(gated, out_matrix, 1, 1)
    branch, cotangent_late = tie((branch.astype(BF16), cotangent))
    back_feed = both_cores(cotangent_late.astype(BF16))
    branch, back_feed = tie((exchange(branch.reshape(4, tokens, D), "y"), back_feed))
    middle = own_tokens(block_input) + jnp.sum(branch.astype(F32), axis=0)
    unit_two, inverse_two, normed_value_two = normalize(middle, norm_gains[1])
    grad_active = dot(back_feed, down_matrix, 1, 0)
    normed_two = normed_value_two.astype(BF16)
    passing, rest = gather_first(normed_two, along("y"), tokens // 2)
    blocks = gather_passed(normed_two, passing, rest, along("y"))
    blocks, grad_active = tie((blocks, grad_active))
    normed_two = ring_order(
        blocks,
        index_along("y"),
        tokens // 2,
        "order_tokens",
    )
    normed_two = both_cores(normed_two.reshape(rows_here, D))
    gate_pre = dot(normed_two, gate_matrix, 1, 0)
    upward = dot(normed_two, up_matrix, 1, 0)
    sigmoid_gate = jax.nn.sigmoid(gate_pre)
    silu_gate = gate_pre * sigmoid_gate
    active = (silu_gate * upward).astype(BF16)

    grad_gate = (
        grad_active * upward * (sigmoid_gate * (1.0 + gate_pre * (1.0 - sigmoid_gate)))
    ).astype(BF16)
    grad_upward = (grad_active * silu_gate).astype(BF16)
    grad_gate_up = jnp.concatenate([grad_gate, grad_upward], axis=1)
    partial = dot(grad_gate_up, gate_up_matrix, 1, 1)
    other, active, grad_gate_up = tie(
        (send(partial[rows_here:].astype(BF16), "core", 1), active, grad_gate_up)
    )
    normed_sums = (partial[:rows_here] + other.astype(F32)).astype(BF16)
    (second_full,) = in_vmem(
        functools.partial(weight_grads_kernel, 4 * LANES),
        [normed_two, back_feed, grad_gate_up, active],
        [jax.ShapeDtypeStruct((D, 3 * half), BF16)],
        "weight_grads",
    )
    normed_sums, second_full = tie(
        (exchange(normed_sums.reshape(4, tokens, D), "y"), second_full)
    )
    feed_partial = dot(active, down_matrix, 1, 1)
    normed_sums, feed_partial = tie((normed_sums, feed_partial))
    second_sum = lax.psum_scatter(second_full, chips, scatter_dimension=0, tiled=True)
    grad_normed_two = jnp.sum(normed_sums.astype(F32), axis=0)
    grad_middle = own_tokens(cotangent) + norm_back(
        grad_normed_two, unit_two, inverse_two, norm_gains[1]
    )
    back_branch = grad_middle.astype(BF16)
    feed_here = core_scatter(feed_partial)
    passing, rest = gather_first(back_branch, along("y"), tokens // 2)
    blocks = gather_passed(back_branch, passing, rest, along("y"))
    blocks, feed_here = tie((blocks, feed_here.astype(BF16)))
    back_branch = ring_order(
        blocks, index_along("y"), tokens // 2, "order_back"
    ).reshape(rows_here, D)

    def own_rows(summed):
        kept = chosen(zero, summed[:owned], summed[owned:])
        return kept, send(chosen(zero, summed[owned:], summed[:owned]), "core", 1)

    second_kept, second_given = own_rows(second_sum)

    out_grad_full = dot(back_branch, gated, 0, 0).astype(BF16)
    grad_gated = dot(back_branch, out_matrix, 1, 0)
    grad_c = grad_gated * convolved
    grad_conv = grad_gated * c_part
    later = shifted(grad_conv[:halo_rows], seq_axes, -1) * has_after
    extended = jnp.concatenate([grad_conv, later], axis=0)
    grad_product = conv_weight[0] * extended[halo_rows : halo_rows + rows_here]
    for offset in range(1, KERNEL):
        grad_product = (
            grad_product
            + conv_weight[offset] * extended[halo_rows - offset : halo_rows - offset + rows_here]
        )
    conv_part = jnp.concatenate(
        [
            jnp.sum(grad_conv * padded[offset : offset + rows_here], axis=0, keepdims=True)
            for offset in range(KERNEL)
        ]
    )
    grad_low = jnp.concatenate([grad_product * x_part, grad_c], axis=1).astype(BF16)
    grad_high = (grad_product * b_part).astype(BF16)
    first_grad_low = dot(normed, grad_low, 0, 0).astype(BF16)
    first_grad_high = jnp.concatenate(
        [dot(normed, grad_high, 0, 0).astype(BF16), out_grad_full], axis=1
    )
    first_other = send(chosen(zero, first_grad_high, first_grad_low), "core", 1)

    wide_high = jnp.concatenate([grad_high, jnp.zeros_like(grad_high)], axis=1)
    grad_normed_here = dot(chosen(zero, grad_low, wide_high), first_kept, 1, 1) + dot(
        chosen(zero, wide_high, grad_low), first_given, 1, 1
    )
    (both,) = in_vmem(
        both_kernel,
        [feed_here, grad_normed_here],
        [jax.ShapeDtypeStruct((4, 2, tokens, D), BF16)],
        "both_pieces",
    )
    first_other, both = tie((first_other, both))
    both = exchange(both, "y")
    first_sum = chosen(zero, first_grad_low, first_grad_high).astype(F32) + first_other.astype(F32)
    first_sum = first_sum.astype(BF16).reshape(4, 4, pair, 2 * width)
    first_sum = chosen(zero, first_sum, jnp.swapaxes(first_sum, 0, 1))
    piece = by_index(first_sum, index_turning(True))
    far, rest = scatter_first(piece, turning(True), 0, 2)
    far, grad_normed_here, grad_normed_two, in_rows, in_cols, late = tie(
        (
            far,
            grad_normed_here,
            grad_normed_two,
            in_rows,
            in_cols,
            (gate_weight, up_weight, down_weight, in_weight, out_weight),
        )
    )

    turned = (False, True, False, False, True)
    cross_full = (3 * D, D, FF, FF, FF)

    def row(x):
        x = x.reshape(1, -1) if x.ndim == 1 else x
        return jnp.pad(x, ((0, 0), (0, hidden - x.shape[1])))

    line_states = in_lanes(
        [state[:, None] for state in (in_rows, out_cols, gate_rows, up_rows, down_cols)]
    )
    cross_states = jnp.concatenate(
        [
            row(jnp.concatenate([in_cols.reshape(3 * width), out_rows])),
            row(gate_cols),
            row(up_cols),
            row(down_rows),
            jnp.zeros((2, hidden), F32),
            row(conv_moment.reshape(KERNEL * width)),
            jnp.zeros((1, hidden), F32),
        ],
        axis=0,
    )
    first_weight = jnp.concatenate([late[3].reshape(owned, 3 * width), late[4].T], axis=1)
    (early,) = in_vmem(
        functools.partial(early_kernel, turned, width),
        [first_weight, late[0], late[1], late[2].T, conv_weight, line_states, cross_states],
        [jax.ShapeDtypeStruct((8, LANES), F32)],
        "early_sums",
    )

    gain_part = jnp.concatenate(
        [
            jnp.sum(grad_normed_here * unit_one, axis=0, keepdims=True),
            jnp.sum(grad_normed_two * unit_two, axis=0, keepdims=True),
        ]
    )
    passed, gain_part = tie((scatter_passed(piece, far, turning(True), 0, 2), gain_part))
    piece = by_index(scatter_joined(piece, passed, rest, 0), index_turning(False))
    far = scatter_far(piece, turning(False), 0, owned)
    far, both = tie((far, both))
    both = jnp.sum(both.astype(F32), axis=0)
    result_here = middle + both[0]
    grad_normed = both[1]
    input_grad_here = grad_middle + norm_back(
        grad_normed, own_tokens(unit_one), own_tokens(inverse_one), norm_gains[0]
    )
    both_here = jnp.concatenate([result_here, input_grad_here], axis=1).astype(BF16)
    near = scatter_near(piece, far, turning(False), 0, owned)
    near, both_here = tie((near, both_here))
    both_full = lax.all_gather(both_here, "y", axis=0, tiled=True)
    first_own, first_other = own_rows(scatter_sum(piece, near).astype(BF16))

    def f32(*shape):
        return jax.ShapeDtypeStruct(shape, F32)

    first_grad, gate_grad, up_grad, down_grad, lines, crosses = in_vmem(
        functools.partial(squares_kernel, half),
        [first_own, first_other, second_kept, second_given, conv_part, gain_part],
        [f32(owned, 4 * width)] + [f32(owned, hidden)] * 3 + [f32(owned, LANES), f32(8, hidden)],
        "square_sums",
    )
    crosses = all_sum(crosses, "x")
    crosses, lines = tie((all_sum(crosses, "z"), all_sum(lines, "y")))
    crosses = crosses + send(crosses, "core", 1)
    conv_grad = crosses[6, : KERNEL * width].reshape(KERNEL, width)
    line_new, cross_new, conv_update, *updates, terms = in_vmem(
        functools.partial(
            with_refs, functools.partial(moments_kernel, width, cross_full), 9
        ),
        [lines, line_states, crosses, cross_states, early, first_grad, gate_grad, up_grad]
        + [down_grad],
        [f32(owned, LANES), f32(8, hidden), f32(KERNEL, width), f32(owned, 4 * width)]
        + [f32(owned, hidden)] * 3
        + [f32(8, LANES)],
        "moments",
    )
    every = ("x", "z", "core", "y")
    terms, gain_parts = tie((terms, crosses[4:6, :D]))
    gain_sums = all_sum(gain_parts, "y")
    sums, both_full = tie((spread(terms[:4].reshape(4 * LANES), every), both_full))
    result = both_full[:, :D].astype(F32)
    input_grad = both_full[:, D:].astype(F32)
    gain_sums, sums = tie((gain_sums, sums))
    sums = jnp.sum(sums, axis=0).reshape(4, LANES)
    conv_new, gain_new, gain_moment_new, gain_grad, *news = in_vmem(
        functools.partial(
            with_refs, functools.partial(weights_kernel, width, cross_full, turned), 14
        ),
        [sums, gain_sums, conv_weight, conv_update, norm_gains, gain_moment]
        + [first_weight, late[0], late[1], late[2].T, *updates],
        [f32(KERNEL, width), f32(2, D), f32(2, D), f32(2, D), f32(owned, 4 * width)]
        + [f32(owned, hidden)] * 3,
        "new_weights",
    )
    in_grad, out_grad = first_grad[:, : 3 * width], first_grad[:, 3 * width :]
    in_new, out_new = news[0][:, : 3 * width], news[0][:, 3 * width :]
    in_cols_new = cross_new[0, : 3 * width]
    out_rows_new = cross_new[0, 3 * width : 4 * width]
    conv_moment_new = cross_new[6, : KERNEL * width].reshape(KERNEL, width)
    return (
        result,
        input_grad,
        in_grad.reshape(in_weight.shape),
        out_grad.T,
        gate_grad,
        up_grad,
        down_grad.T,
        conv_grad,
        gain_grad,
        in_new.reshape(in_weight.shape),
        out_new.T,
        news[1],
        news[2],
        news[3].T,
        conv_new,
        gain_new,
        line_new[:, 0],
        in_cols_new.reshape(in_cols.shape),
        out_rows_new,
        line_new[:, 1],
        line_new[:, 2],
        cross_new[1],
        line_new[:, 3],
        cross_new[2],
        cross_new[3],
        line_new[:, 4],
        conv_moment_new,
        gain_moment_new,
    )


def solution(mesh):
    seq = ("x", "z", "core")
    model = "y"
    inner = Mesh(mesh.devices.reshape(4, 4, 2, 4), ("x", "z", "core", "y"))
    in_specs = (
        P(seq, None),
        P(seq, None),
        P(),
        P(None, model),
        P(seq, None, model),
        P(model, seq),
        P(seq, model),
        P(seq, model),
        P(model, seq),
        P(seq),
        P(None, model),
        P(model),
        P(seq),
        P(seq),
        P(model),
        P(seq),
        P(model),
        P(model),
        P(seq),
        P(None, model),
        P(),
    )
    out_specs = (
        P(seq, None),
        P(seq, None),
        P(seq, None, model),
        P(model, seq),
        P(seq, model),
        P(seq, model),
        P(model, seq),
        P(None, model),
        P(),
        P(seq, None, model),
        P(model, seq),
        P(seq, model),
        P(seq, model),
        P(model, seq),
        P(None, model),
        P(),
        P(seq),
        P(None, model),
        P(model),
        P(seq),
        P(seq),
        P(model),
        P(seq),
        P(model),
        P(model),
        P(seq),
        P(None, model),
        P(),
    )
    return jax.shard_map(
        on_device, mesh=inner, in_specs=in_specs, out_specs=out_specs, check_vma=False
    )
```

```python
import functools

import jax
import jax.numpy as jnp
from jax import lax
from jax.experimental import pallas as pl
from jax.experimental.pallas import tpu as pltpu
from jax.sharding import Mesh
from jax.sharding import PartitionSpec as P

D = 1536
FF = 6912
KERNEL = 3
SEQS = 2

NORM_EPS = 1e-05
DECAY_RATE = 0.5
SQUARE_EPS = 1e-30
CLIP_LIMIT = 0.2
STEP_RATE = 4.0

BF16 = jnp.bfloat16
F32 = jnp.float32
LANES = 128


def send(x, axis, by):
    size = lax.axis_size(axis)
    return lax.ppermute(x, axis, [(i, (i + by) % size) for i in range(size)])


def shifted(x, axis, by):
    size = lax.axis_size(axis)
    pairs = [(i, i + by) for i in range(size) if 0 <= i + by < size]
    return lax.ppermute(x, axis, pairs)


def dot(left_side, right_side, left_axis, right_axis):
    return lax.dot_general(
        left_side,
        right_side,
        (((left_axis,), (right_axis,)), ((), ())),
        preferred_element_type=F32,
    )


def exchange(x, axes):
    return lax.all_to_all(x, axes, split_axis=0, concat_axis=0, tiled=True)


def spread(x, axes):
    return exchange(jnp.broadcast_to(x, (lax.axis_size(axes), *x.shape)), axes)


def halves(x, axis, cut):
    size = x.shape[axis]
    return (
        lax.slice_in_dim(x, 0, cut, axis=axis),
        lax.slice_in_dim(x, cut, size, axis=axis),
    )


def send_turned(x, turned, by):
    pairs = []
    for i in range(32):
        at = [i // 8, i // 2 % 4]
        axis = (1 - i % 2) ^ turned
        at[axis] = (at[axis] + by) % 4
        pairs.append((i, at[0] * 8 + at[1] * 2 + i % 2))
    return lax.ppermute(x, ("x", "z", "core"), pairs)


def gather_near(block, send_by):
    return send_by(block, 1), send_by(block, -1)


def gather_far(block, near, send_by, cut):
    before, after = near
    return block, after, send_by(before[:cut], 1), send_by(after[cut:], -1), before


def ring_gather(block, send_by, cut):
    return gather_far(block, gather_near(block, send_by), send_by, cut)


def gather_first(block, send_by, cut):
    first, second = block[:cut], block[cut:]
    passing = send_by(first, 1), send_by(second, -1)
    return passing, (send_by(second, 1), send_by(first, -1))


def gather_passed(block, passing, rest, send_by):
    far = send_by(passing[0], 1), send_by(passing[1], -1)
    return block, rest[1], passing[1], far[0], far[1], passing[0], rest[0]


def along(axis):
    return lambda x, by: send(x, axis, by)


def turning(turned):
    return lambda x, by: send_turned(x, turned, by)


def in_vmem(kernel, arrays, out_shapes, name):
    moved = sum(a.size * a.dtype.itemsize for a in arrays) + sum(
        o.size * o.dtype.itemsize for o in out_shapes
    )
    return pl.pallas_call(
        kernel,
        out_shape=out_shapes,
        in_specs=[pl.BlockSpec(memory_space=pltpu.VMEM)] * len(arrays),
        out_specs=[pl.BlockSpec(memory_space=pltpu.VMEM)] * len(out_shapes),
        compiler_params=pltpu.CompilerParams(vmem_limit_bytes=2 * moved + 8 * 2**20),
        cost_estimate=pl.CostEstimate(flops=0, bytes_accessed=moved, transcendentals=0),
        name=name,
    )(*arrays)


def ring_places(here):
    return [(here + by) & 3 for by in (0, 1, 2, 2, 3)]


def ring_kernel(index, cut, *refs):
    out = refs[5]
    for at, (place, ref) in enumerate(zip(ring_places(index()), refs[:5])):
        if at == 2:
            out[place, :cut] = ref[...]
        elif at == 3:
            out[place, cut:] = ref[...]
        else:
            out[place] = ref[...]


def ring_parts_kernel(index, cut, *refs):
    out = refs[7]
    here = index()
    out[here] = refs[0][...]
    for by in (1, 2, 3):
        out[(here + by) & 3, :cut] = refs[2 * by - 1][...]
        out[(here + by) & 3, cut:] = refs[2 * by][...]


def ring_order(blocks, index, cut, name):
    shape = jax.ShapeDtypeStruct((4, *blocks[0].shape), blocks[0].dtype)
    kernel = ring_kernel if len(blocks) == 5 else ring_parts_kernel
    return in_vmem(functools.partial(kernel, index, cut), blocks, [shape], name)[0]


def index_along(axis):
    return lambda: lax.axis_index(axis)


def index_turning(turned):
    def index():
        on_z = (lax.axis_index("core") == 0) != turned
        return jnp.where(on_z, lax.axis_index("z"), lax.axis_index("x"))

    return index


def stack_kernel(*refs):
    out = refs[-1]
    start = 0
    for ref in refs[:-1]:
        out[start : start + ref.shape[0]] = ref[...]
        start += ref.shape[0]


def stacked(blocks, name):
    rows = sum(block.shape[0] for block in blocks)
    shape = jax.ShapeDtypeStruct((rows, blocks[0].shape[1]), blocks[0].dtype)
    return in_vmem(stack_kernel, blocks, [shape], name)[0]


def weight_grads_kernel(rows, normed, back, grad_gate_up, active, out):
    wide = grad_gate_up.shape[1]

    @pl.loop(0, normed.shape[1] // rows)
    def _(at):
        part = pl.ds(pl.multiple_of(at * rows, rows), rows)
        left = normed[:, part]
        out[part, :wide] = dot(left, grad_gate_up[...], 0, 0).astype(BF16)
        out[part, wide:] = dot(back[:, part], active[...], 0, 0).astype(BF16)


def chips_kernel(*refs):
    out = refs[5]
    zero = lax.axis_index("core") == 0
    for is_zero in (True, False):

        @pl.when(zero == is_zero)
        def _():
            places = ring_places(lax.axis_index("x" if is_zero else "z"))
            for at, (place, ref) in enumerate(zip(places, refs[:5])):
                cut = {2: slice(0, 2), 3: slice(2, 4)}.get(at, slice(0, 4))
                if is_zero:
                    out[place, cut] = ref[...]
                else:
                    out[cut, place] = ref[...]


def both_kernel(feed, grad, out):
    out[:, 0] = feed[...].reshape(out.shape[0], out.shape[2], out.shape[3])
    out[:, 1] = grad[...].astype(BF16).reshape(out.shape[0], out.shape[2], out.shape[3])


def by_index(pieces, index):
    here = index()
    return lambda by: lax.dynamic_index_in_dim(pieces, (here + by) & 3, 0, keepdims=False)


tie = lax.optimization_barrier


def scatter_far(piece, send_by, along, cut):
    far_first, far_second = halves(piece(2).astype(BF16), along, cut)
    return send_by(far_first, 1), send_by(far_second, -1)


def scatter_near(piece, far, send_by, along, cut):
    from_before, from_after = far
    up_first, up_second = halves(piece(1), along, cut)
    down_first, down_second = halves(piece(3), along, cut)
    upward = jnp.concatenate(
        [(up_first.astype(F32) + from_before.astype(F32)).astype(BF16), up_second.astype(BF16)],
        axis=along,
    )
    downward = jnp.concatenate(
        [down_first.astype(BF16), (down_second.astype(F32) + from_after.astype(F32)).astype(BF16)],
        axis=along,
    )
    return send_by(upward, 1), send_by(downward, -1)


def scatter_first(piece, send_by, along, cut):
    far = scatter_far(piece, send_by, along, cut)
    up = halves(piece(1), along, cut)[1].astype(BF16)
    down = halves(piece(3), along, cut)[0].astype(BF16)
    return far, (send_by(up, 1), send_by(down, -1))


def scatter_passed(piece, far, send_by, along, cut):
    up = halves(piece(1), along, cut)[0].astype(F32) + far[0].astype(F32)
    down = halves(piece(3), along, cut)[1].astype(F32) + far[1].astype(F32)
    return send_by(up.astype(BF16), 1), send_by(down.astype(BF16), -1)


def scatter_joined(piece, passed, rest, along):
    from_before = jnp.concatenate([passed[0], rest[0]], axis=along)
    from_after = jnp.concatenate([rest[1], passed[1]], axis=along)
    return scatter_sum(piece, (from_before, from_after))


def scatter_sum(piece, near):
    return piece(0).astype(F32) + (near[0].astype(F32) + near[1].astype(F32))


def all_sum(x, axis):
    return (x + send(x, axis, 2)) + (send(x, axis, 1) + send(x, axis, -1))


def seq_sum(x):
    x = all_sum(all_sum(x, "x"), "z")
    return x + send(x, "core", 1)


def normalize(values, gain_row):
    inverse = lax.rsqrt(jnp.mean(values * values, axis=1, keepdims=True) + NORM_EPS)
    unit_rows = values * inverse
    return (unit_rows, inverse, unit_rows * gain_row)


def norm_back(upstream, unit_rows, inverse, gain_row):
    scaled = upstream * gain_row
    return inverse * (scaled - unit_rows * jnp.mean(scaled * unit_rows, axis=1, keepdims=True))


def chosen(first, yes, no):
    return jnp.where(first, yes, no)


def in_lanes(columns):
    lane = lax.broadcasted_iota(jnp.int32, (1, LANES), 1)
    return sum(jnp.where(lane == at, column, 0.0) for at, column in enumerate(columns))


def in_rows_of(rows):
    line = lax.broadcasted_iota(jnp.int32, (8, 1), 0)
    return sum(jnp.where(line == at, r, 0.0) for at, r in rows.items())


def total(x):
    return jnp.sum(jnp.sum(x, axis=0, keepdims=True), axis=1, keepdims=True)


def flag(axes):
    first = functools.reduce(jnp.logical_and, [lax.axis_index(axis) == 0 for axis in axes])
    return jnp.where(first, 1.0, 0.0)


def sizes_in_lanes(sizes):
    return in_lanes([jnp.full((1, 1), size, F32) for size in sizes])


def early_kernel(turned, width, first, gate, up, down, conv, lines, crosses, out):
    seq_first, model_first = flag(("x", "z", "core")), flag(("y",))
    split = 3 * width
    weights = [first[:, :split], first[:, split:], gate[...], up[...], down[...]]
    squares = [total(w * w) for w in weights] + [total(conv[...] * conv[...]) * seq_first]
    cross_rows = [crosses[0:1, :split], crosses[0:1, split : split + width]]
    cross_rows += [crosses[at : at + 1, :] for at in (1, 2, 3)]
    moments = [
        total(cross_rows[at]) * seq_first
        if turned[at]
        else total(lines[:, at : at + 1]) * model_first
        for at in range(5)
    ]
    out[...] = in_rows_of({1: in_lanes(squares), 3: in_lanes(moments)})


def squares_kernel(
    half, first_kept, first_given, kept, given, conv, gain, first, gate, up, down, lines, crosses
):
    zero = lax.axis_index("core") == 0
    wide = first_kept.shape[1]
    low = jnp.where(zero, first_kept[...], first_given[...]).astype(F32)
    high = jnp.where(zero, first_given[...], first_kept[...]).astype(F32)
    first[:, :wide] = low
    first[:, wide:] = high
    rest = gate.shape[1] - half
    for at, ref in enumerate((gate, up, down)):
        cols = slice(at * half, (at + 1) * half)
        low = jnp.where(zero, kept[:, cols], given[:, cols]).astype(F32)
        high = jnp.where(zero, given[:, cols], kept[:, cols]).astype(F32)
        ref[:, :half] = low
        ref[:, half:] = high[:, :rest]
    split = 3 * (wide // 2)
    crosses[...] = jnp.zeros_like(crosses)
    sums = []
    parts = [(0, 0, first[:, :split]), (0, split, first[:, split:])]
    parts += [(1, 0, gate[...]), (2, 0, up[...]), (3, 0, down[...])]
    for row, start, grad in parts:
        square = grad * grad + SQUARE_EPS
        sums.append(jnp.sum(square, axis=1, keepdims=True))
        crosses[row : row + 1, start : start + grad.shape[1]] = jnp.sum(
            square, axis=0, keepdims=True
        )
    lines[...] = in_lanes(sums)
    crosses[4:6, : gain.shape[1]] = gain[...]
    width = conv.shape[1]
    for tap in range(KERNEL):
        crosses[6:7, tap * width : (tap + 1) * width] = conv[tap : tap + 1, :]


def moments_kernel(width, cross_full, refs_in, refs_out):
    lines, line_states, crosses, cross_states, early, first, gate, up, down = refs_in
    new_lines, new_crosses, conv_update, u_first, u_gate, u_up, u_down, terms = refs_out
    seq_first, model_first = flag(("x", "z", "core")), flag(("y",))
    line_mean = lines[...] / sizes_in_lanes([*cross_full, *[1.0] * (LANES - 5)][:8])
    lane = lax.broadcasted_iota(jnp.int32, (1, LANES), 1)
    line_mean = jnp.where(lane < 5, line_mean, 0.0)
    fresh = DECAY_RATE * line_states[...] + (1.0 - DECAY_RATE) * line_mean
    new_lines[...] = fresh
    across = DECAY_RATE * cross_states[0:4, :] + (1.0 - DECAY_RATE) * (crosses[0:4, :] / D)
    new_crosses[...] = jnp.zeros_like(new_crosses)
    new_crosses[0:4, :] = across
    conv_grad = crosses[6:7, : KERNEL * width]
    conv_moment = DECAY_RATE * cross_states[6:7, : KERNEL * width] + (1.0 - DECAY_RATE) * (
        conv_grad * conv_grad + SQUARE_EPS
    )
    new_crosses[6:7, : KERNEL * width] = conv_moment
    moved = conv_grad * lax.rsqrt(conv_moment)
    for tap in range(KERNEL):
        conv_update[tap : tap + 1, :] = moved[:, tap * width : (tap + 1) * width]
    split = 3 * width
    sums = []
    for slot, (grad, out, row, cols) in enumerate(
        (
            (first, u_first, 0, slice(0, split)),
            (first, u_first, 0, slice(split, split + width)),
            (gate, u_gate, 1, slice(None)),
            (up, u_up, 2, slice(None)),
            (down, u_down, 3, slice(None)),
        )
    ):
        second = fresh[:, slot : slot + 1] * across[row : row + 1, cols]
        update = grad[:, cols] * lax.rsqrt(second)
        out[:, cols] = update
        sums.append(total(update * update))
    sums.append(total(moved * moved) * seq_first)
    squares = jnp.sum(lines[...], axis=0, keepdims=True) * model_first
    terms[...] = early[...] + in_rows_of({0: in_lanes(sums), 2: squares})


def weights_kernel(width, cross_full, turned, refs_in, refs_out):
    sums, gain_sums, conv, conv_update, gains, gain_moment, *rest = refs_in
    weights, updates = rest[:4], rest[4:]
    conv_new, gains_new, gain_moment_new, gain_grad, *news = refs_out
    rows = [full if turn else D for full, turn in zip(cross_full, turned)]
    cols = [D if turn else full for full, turn in zip(cross_full, turned)]
    lane = lax.broadcasted_iota(jnp.int32, (1, LANES), 1)
    rows_lane = jnp.where(lane < 5, sizes_in_lanes(rows), 1.0)
    cols_lane = jnp.where(lane < 5, sizes_in_lanes(cols), 1.0)
    counts = jnp.where(lane < 5, rows_lane * cols_lane, float(KERNEL * D))
    table = sums[...]
    row_mean = (
        DECAY_RATE * table[3:4] + (1.0 - DECAY_RATE) * (table[2:3] / cols_lane)
    ) / rows_lane
    row_mean = jnp.where(lane < 5, row_mean, 1.0)
    update_rms = jnp.sqrt(row_mean * (table[0:1] / counts))
    weight_rms = jnp.sqrt(table[1:2] / counts)
    factor = STEP_RATE * weight_rms / jnp.maximum(1.0, update_rms / CLIP_LIMIT)
    factor = factor * jnp.sqrt(row_mean)
    split = 3 * width
    for slot, (at, part) in enumerate(
        (
            (0, slice(0, split)),
            (0, slice(split, split + width)),
            (1, slice(None)),
            (2, slice(None)),
            (3, slice(None)),
        )
    ):
        news[at][:, part] = (
            weights[at][:, part] - factor[:, slot : slot + 1] * updates[at][:, part]
        )
    conv_new[...] = conv[...] - factor[:, 5:6] * conv_update[...]
    grad = gain_sums[...]
    gain_grad[...] = grad
    moment = DECAY_RATE * gain_moment[...] + (1.0 - DECAY_RATE) * (grad * grad + SQUARE_EPS)
    gain_moment_new[...] = moment
    update = grad * lax.rsqrt(moment)
    count = float(D)
    update_rms = jnp.sqrt(jnp.sum(update * update, axis=1, keepdims=True) / count)
    weight_rms = jnp.sqrt(jnp.sum(gains[...] * gains[...], axis=1, keepdims=True) / count)
    gains_new[...] = gains[...] - STEP_RATE * weight_rms * (
        update / jnp.maximum(1.0, update_rms / CLIP_LIMIT)
    )


def with_refs(kernel, n_in, *refs):
    kernel(refs[:n_in], refs[n_in:])


def on_device(
    block_input,
    cotangent,
    norm_gains,
    conv_weight,
    in_weight,
    out_weight,
    gate_weight,
    up_weight,
    down_weight,
    in_rows,
    in_cols,
    out_rows,
    out_cols,
    gate_rows,
    gate_cols,
    up_rows,
    up_cols,
    down_rows,
    down_cols,
    conv_moment,
    gain_moment,
):
    rows_here = block_input.shape[0]
    width = conv_weight.shape[1]
    owned = in_weight.shape[0]
    hidden = gate_weight.shape[1]
    halo_rows = KERNEL - 1
    seq_axes = ("x", "z", "core")
    core = lax.axis_index("core")
    model = lax.axis_index("y")
    blocks_per_seq = lax.axis_size(seq_axes) // SEQS
    block_place = lax.axis_index(seq_axes) % blocks_per_seq
    has_before = (block_place != 0).astype(F32)
    has_after = (block_place != blocks_per_seq - 1).astype(F32)
    tokens = rows_here // 4

    in_flat = in_weight.reshape(owned, 3 * width)
    out_turned = out_weight.T
    down_turned = down_weight.T

    zero = core == 0
    chips = ("x", "z")
    pair = 2 * owned

    def both_rows(low, high):
        kept = chosen(zero, low, high)
        given = send(chosen(zero, high, low), "core", 1)
        return jnp.concatenate(
            [chosen(zero, kept, given), chosen(zero, given, kept)], axis=0
        ), given

    in_bf16 = in_flat.astype(BF16)
    first_shard, given = both_rows(
        in_bf16[:, : 2 * width],
        jnp.concatenate([in_bf16[:, 2 * width :], out_turned.astype(BF16)], axis=1),
    )
    part = ring_gather(first_shard, turning(False), owned)

    second, given = tie(((gate_weight, up_weight, down_weight), given))
    padded_hidden = -(-hidden // (2 * LANES)) * 2 * LANES
    half = padded_hidden // 2
    second = [
        jnp.pad(w.astype(BF16), ((0, 0), (0, padded_hidden - hidden)))
        for w in (second[0], second[1], second[2].T)
    ]
    second_shard, _ = both_rows(
        jnp.concatenate([w[:, :half] for w in second], axis=1),
        jnp.concatenate([w[:, half:] for w in second], axis=1),
    )

    part = ring_order(part, index_turning(False), owned, "order_first")
    unit_one, inverse_one, normed_value = normalize(block_input, norm_gains[0])
    near, second_shard = tie((gather_near(part, turning(True)), second_shard))
    second_matrix = lax.all_gather(second_shard, chips, axis=0, tiled=True)
    gate_matrix = second_matrix[:, :half]
    up_matrix = second_matrix[:, half : 2 * half]
    gate_up_matrix = second_matrix[:, : 2 * half]
    down_matrix = second_matrix[:, 2 * half :]
    (first_kept,) = in_vmem(
        chips_kernel,
        gather_far(part, near, turning(True), 2),
        [jax.ShapeDtypeStruct((4, 4, pair, 2 * width), BF16)],
        "order_chips",
    )
    first_kept = first_kept.reshape(D, 2 * width)
    first_given = send(first_kept, "core", 1)
    out_matrix = chosen(zero, first_given[:, width:], first_kept[:, width:])

    def own_tokens(x):
        return lax.dynamic_slice_in_dim(x, model * tokens, tokens, axis=0)

    def piece_of(x):
        return by_index(x.reshape(4, tokens, D), index_along("y"))

    def both_cores(x):
        return stacked([x, send(x, "core", 1)], "both_cores")

    def core_scatter(partial):
        other = send(partial[rows_here:].astype(BF16), "core", 1)
        return partial[:rows_here] + other.astype(F32)

    normed = normed_value.astype(BF16)
    projected_kept = dot(normed, first_kept, 1, 0)
    projected_given = dot(normed, first_given, 1, 0)
    b_part = chosen(zero, projected_kept[:, :width], projected_given[:, :width])
    c_part = chosen(zero, projected_kept[:, width:], projected_given[:, width:])
    x_part = chosen(zero, projected_given[:, :width], projected_kept[:, :width])
    product = b_part * x_part
    earlier = shifted(product[rows_here - halo_rows :], seq_axes, 1) * has_before
    padded = jnp.concatenate([earlier, product], axis=0)
    convolved = conv_weight[0] * padded[0:rows_here]
    for offset in range(1, KERNEL):
        convolved = convolved + conv_weight[offset] * padded[offset : offset + rows_here]
    gated = (c_part * convolved).astype(BF16)
    branch = dot(gated, out_matrix, 1, 1)
    branch, cotangent_late = tie((branch.astype(BF16), cotangent))
    back_feed = both_cores(cotangent_late.astype(BF16))
    branch, back_feed = tie((exchange(branch.reshape(4, tokens, D), "y"), back_feed))
    middle = own_tokens(block_input) + jnp.sum(branch.astype(F32), axis=0)
    unit_two, inverse_two, normed_value_two = normalize(middle, norm_gains[1])
    grad_active = dot(back_feed, down_matrix, 1, 0)
    normed_two = normed_value_two.astype(BF16)
    passing, rest = gather_first(normed_two, along("y"), tokens // 2)
    blocks = gather_passed(normed_two, passing, rest, along("y"))
    normed_two = ring_order(
        blocks,
        index_along("y"),
        tokens // 2,
        "order_tokens",
    )
    normed_two = normed_two.reshape(rows_here, D)
    other, grad_active = tie((send(normed_two, "core", 1), grad_active))
    normed_two = stacked([normed_two, other], "both_cores")
    gate_pre = dot(normed_two, gate_matrix, 1, 0)
    upward = dot(normed_two, up_matrix, 1, 0)
    sigmoid_gate = jax.nn.sigmoid(gate_pre)
    silu_gate = gate_pre * sigmoid_gate
    active = (silu_gate * upward).astype(BF16)

    grad_gate = (
        grad_active * upward * (sigmoid_gate * (1.0 + gate_pre * (1.0 - sigmoid_gate)))
    ).astype(BF16)
    grad_upward = (grad_active * silu_gate).astype(BF16)
    grad_gate_up = jnp.concatenate([grad_gate, grad_upward], axis=1)
    partial = dot(grad_gate_up, gate_up_matrix, 1, 1)
    other, active, grad_gate_up = tie(
        (send(partial[rows_here:].astype(BF16), "core", 1), active, grad_gate_up)
    )
    normed_sums = (partial[:rows_here] + other.astype(F32)).astype(BF16)
    (second_full,) = in_vmem(
        functools.partial(weight_grads_kernel, 4 * LANES),
        [normed_two, back_feed, grad_gate_up, active],
        [jax.ShapeDtypeStruct((D, 3 * half), BF16)],
        "weight_grads",
    )
    normed_sums, second_full = tie(
        (exchange(normed_sums.reshape(4, tokens, D), "y"), second_full)
    )
    feed_partial = dot(active, down_matrix, 1, 1)
    normed_sums, feed_partial = tie((normed_sums, feed_partial))
    second_sum = lax.psum_scatter(second_full, chips, scatter_dimension=0, tiled=True)
    grad_normed_two = jnp.sum(normed_sums.astype(F32), axis=0)
    grad_middle = own_tokens(cotangent) + norm_back(
        grad_normed_two, unit_two, inverse_two, norm_gains[1]
    )
    back_branch = grad_middle.astype(BF16)
    feed_here = core_scatter(feed_partial)
    passing, rest = gather_first(back_branch, along("y"), tokens // 2)
    blocks = gather_passed(back_branch, passing, rest, along("y"))
    blocks, feed_here = tie((blocks, feed_here.astype(BF16)))
    back_branch = ring_order(
        blocks, index_along("y"), tokens // 2, "order_back"
    ).reshape(rows_here, D)

    def own_rows(summed):
        kept = chosen(zero, summed[:owned], summed[owned:])
        return kept, send(chosen(zero, summed[owned:], summed[:owned]), "core", 1)

    second_kept, second_given = own_rows(second_sum)

    out_grad_full = dot(back_branch, gated, 0, 0).astype(BF16)
    grad_gated = dot(back_branch, out_matrix, 1, 0)
    grad_c = grad_gated * convolved
    grad_conv = grad_gated * c_part
    later = shifted(grad_conv[:halo_rows], seq_axes, -1) * has_after
    extended = jnp.concatenate([grad_conv, later], axis=0)
    grad_product = conv_weight[0] * extended[halo_rows : halo_rows + rows_here]
    for offset in range(1, KERNEL):
        grad_product = (
            grad_product
            + conv_weight[offset] * extended[halo_rows - offset : halo_rows - offset + rows_here]
        )
    conv_part = jnp.concatenate(
        [
            jnp.sum(grad_conv * padded[offset : offset + rows_here], axis=0, keepdims=True)
            for offset in range(KERNEL)
        ]
    )
    grad_low = jnp.concatenate([grad_product * x_part, grad_c], axis=1).astype(BF16)
    grad_high = (grad_product * b_part).astype(BF16)
    first_grad_low = dot(normed, grad_low, 0, 0).astype(BF16)
    first_grad_high = jnp.concatenate(
        [dot(normed, grad_high, 0, 0).astype(BF16), out_grad_full], axis=1
    )
    first_other = send(chosen(zero, first_grad_high, first_grad_low), "core", 1)

    wide_high = jnp.concatenate([grad_high, jnp.zeros_like(grad_high)], axis=1)
    grad_normed_here = dot(chosen(zero, grad_low, wide_high), first_kept, 1, 1) + dot(
        chosen(zero, wide_high, grad_low), first_given, 1, 1
    )
    (both,) = in_vmem(
        both_kernel,
        [feed_here, grad_normed_here],
        [jax.ShapeDtypeStruct((4, 2, tokens, D), BF16)],
        "both_pieces",
    )
    first_other, both = tie((first_other, both))
    both = exchange(both, "y")
    first_sum = chosen(zero, first_grad_low, first_grad_high).astype(F32) + first_other.astype(F32)
    first_sum = first_sum.astype(BF16).reshape(4, 4, pair, 2 * width)
    first_sum = chosen(zero, first_sum, jnp.swapaxes(first_sum, 0, 1))
    piece = by_index(first_sum, index_turning(True))
    far, rest = scatter_first(piece, turning(True), 0, 2)
    far, grad_normed_here, grad_normed_two, in_rows, in_cols, late = tie(
        (
            far,
            grad_normed_here,
            grad_normed_two,
            in_rows,
            in_cols,
            (gate_weight, up_weight, down_weight, in_weight, out_weight),
        )
    )

    turned = (False, True, False, False, True)
    cross_full = (3 * D, D, FF, FF, FF)

    def row(x):
        x = x.reshape(1, -1) if x.ndim == 1 else x
        return jnp.pad(x, ((0, 0), (0, hidden - x.shape[1])))

    line_states = in_lanes(
        [state[:, None] for state in (in_rows, out_cols, gate_rows, up_rows, down_cols)]
    )
    cross_states = jnp.concatenate(
        [
            row(jnp.concatenate([in_cols.reshape(3 * width), out_rows])),
            row(gate_cols),
            row(up_cols),
            row(down_rows),
            jnp.zeros((2, hidden), F32),
            row(conv_moment.reshape(KERNEL * width)),
            jnp.zeros((1, hidden), F32),
        ],
        axis=0,
    )
    first_weight = jnp.concatenate([late[3].reshape(owned, 3 * width), late[4].T], axis=1)
    (early,) = in_vmem(
        functools.partial(early_kernel, turned, width),
        [first_weight, late[0], late[1], late[2].T, conv_weight, line_states, cross_states],
        [jax.ShapeDtypeStruct((8, LANES), F32)],
        "early_sums",
    )

    gain_part = jnp.concatenate(
        [
            jnp.sum(grad_normed_here * unit_one, axis=0, keepdims=True),
            jnp.sum(grad_normed_two * unit_two, axis=0, keepdims=True),
        ]
    )
    passed, gain_part = tie((scatter_passed(piece, far, turning(True), 0, 2), gain_part))
    piece = by_index(scatter_joined(piece, passed, rest, 0), index_turning(False))
    far = scatter_far(piece, turning(False), 0, owned)
    far, both = tie((far, both))
    both = jnp.sum(both.astype(F32), axis=0)
    result_here = middle + both[0]
    grad_normed = both[1]
    input_grad_here = grad_middle + norm_back(
        grad_normed, own_tokens(unit_one), own_tokens(inverse_one), norm_gains[0]
    )
    both_here = jnp.concatenate([result_here, input_grad_here], axis=1).astype(BF16)
    near = scatter_near(piece, far, turning(False), 0, owned)
    near, both_here = tie((near, both_here))
    both_full = lax.all_gather(both_here, "y", axis=0, tiled=True)
    first_own, first_other = own_rows(scatter_sum(piece, near).astype(BF16))

    def f32(*shape):
        return jax.ShapeDtypeStruct(shape, F32)

    first_grad, gate_grad, up_grad, down_grad, lines, crosses = in_vmem(
        functools.partial(squares_kernel, half),
        [first_own, first_other, second_kept, second_given, conv_part, gain_part],
        [f32(owned, 4 * width)] + [f32(owned, hidden)] * 3 + [f32(owned, LANES), f32(8, hidden)],
        "square_sums",
    )
    crosses = all_sum(crosses, "x")
    crosses, lines = tie((all_sum(crosses, "z"), all_sum(lines, "y")))
    crosses = crosses + send(crosses, "core", 1)
    conv_grad = crosses[6, : KERNEL * width].reshape(KERNEL, width)
    line_new, cross_new, conv_update, *updates, terms = in_vmem(
        functools.partial(
            with_refs, functools.partial(moments_kernel, width, cross_full), 9
        ),
        [lines, line_states, crosses, cross_states, early, first_grad, gate_grad, up_grad]
        + [down_grad],
        [f32(owned, LANES), f32(8, hidden), f32(KERNEL, width), f32(owned, 4 * width)]
        + [f32(owned, hidden)] * 3
        + [f32(8, LANES)],
        "moments",
    )
    every = ("x", "z", "core", "y")
    terms, gain_parts = tie((terms, crosses[4:6, :D]))
    gain_sums = all_sum(gain_parts, "y")
    sums, both_full = tie((spread(terms[:4].reshape(4 * LANES), every), both_full))
    result = both_full[:, :D].astype(F32)
    input_grad = both_full[:, D:].astype(F32)
    gain_sums, sums = tie((gain_sums, sums))
    sums = jnp.sum(sums, axis=0).reshape(4, LANES)
    conv_new, gain_new, gain_moment_new, gain_grad, *news = in_vmem(
        functools.partial(
            with_refs, functools.partial(weights_kernel, width, cross_full, turned), 14
        ),
        [sums, gain_sums, conv_weight, conv_update, norm_gains, gain_moment]
        + [first_weight, late[0], late[1], late[2].T, *updates],
        [f32(KERNEL, width), f32(2, D), f32(2, D), f32(2, D), f32(owned, 4 * width)]
        + [f32(owned, hidden)] * 3,
        "new_weights",
    )
    in_grad, out_grad = first_grad[:, : 3 * width], first_grad[:, 3 * width :]
    in_new, out_new = news[0][:, : 3 * width], news[0][:, 3 * width :]
    in_cols_new = cross_new[0, : 3 * width]
    out_rows_new = cross_new[0, 3 * width : 4 * width]
    conv_moment_new = cross_new[6, : KERNEL * width].reshape(KERNEL, width)
    return (
        result,
        input_grad,
        in_grad.reshape(in_weight.shape),
        out_grad.T,
        gate_grad,
        up_grad,
        down_grad.T,
        conv_grad,
        gain_grad,
        in_new.reshape(in_weight.shape),
        out_new.T,
        news[1],
        news[2],
        news[3].T,
        conv_new,
        gain_new,
        line_new[:, 0],
        in_cols_new.reshape(in_cols.shape),
        out_rows_new,
        line_new[:, 1],
        line_new[:, 2],
        cross_new[1],
        line_new[:, 3],
        cross_new[2],
        cross_new[3],
        line_new[:, 4],
        conv_moment_new,
        gain_moment_new,
    )


def solution(mesh):
    seq = ("x", "z", "core")
    model = "y"
    inner = Mesh(mesh.devices.reshape(4, 4, 2, 4), ("x", "z", "core", "y"))
    in_specs = (
        P(seq, None),
        P(seq, None),
        P(),
        P(None, model),
        P(seq, None, model),
        P(model, seq),
        P(seq, model),
        P(seq, model),
        P(model, seq),
        P(seq),
        P(None, model),
        P(model),
        P(seq),
        P(seq),
        P(model),
        P(seq),
        P(model),
        P(model),
        P(seq),
        P(None, model),
        P(),
    )
    out_specs = (
        P(seq, None),
        P(seq, None),
        P(seq, None, model),
        P(model, seq),
        P(seq, model),
        P(seq, model),
        P(model, seq),
        P(None, model),
        P(),
        P(seq, None, model),
        P(model, seq),
        P(seq, model),
        P(seq, model),
        P(model, seq),
        P(None, model),
        P(),
        P(seq),
        P(None, model),
        P(model),
        P(seq),
        P(seq),
        P(model),
        P(seq),
        P(model),
        P(model),
        P(seq),
        P(None, model),
        P(),
    )
    return jax.shard_map(
        on_device, mesh=inner, in_specs=in_specs, out_specs=out_specs, check_vma=False
    )
```
